512 devices in a mesh: batch: 32 (over y, x, core), proto: 16 (over z).
Axes of the slice: x: 4, y: 4, z: 16, core: 2. Of those that a mesh axis runs over, the one named last changes fastest.
Arguments:
- teacher_feat: bfloat16 [4096, 256], P('batch'), may hold values from -12 to 12
- student_feat: bfloat16 [4096, 256], P('batch'), may hold values from -48 to 48
- teacher_proto: bfloat16 [131072, 256], P(('proto', 'batch')), may hold values from -2 to 2
- student_proto: bfloat16 [131072, 256], P(('proto', 'batch')), may hold values from -0.375 to 0.375
Outputs:
- targets: bfloat16 [4096, 131072], P('batch', 'proto')
- student_grad: float32 [4096, 256], P('batch')
- loss: float32 [], replicated
The draws below stay inside these ranges and needn't reach their ends.
All inputs are finite; a program needn't handle non-finite values.
Results may differ from the reference program's by a relative error of at most 0.004.
Values may be sent and summed in bfloat16 or wider, within the bound.
A program may use at most 128 MiB of HBM per device.

```python
import math
import jax
import jax.numpy as jnp
from jax import lax

D = 256
PROTOS = 131072
ITERS = 3
ROWS = 4096


def shared_features(key):
    return jax.random.normal(jax.random.fold_in(key, 101), (ROWS, D), jnp.float32)


def shared_centers(key):
    return jax.random.normal(jax.random.fold_in(key, 102), (PROTOS, D), jnp.float32)


def proto_factors(key):
    spread = jax.random.uniform(jax.random.fold_in(key, 103), (PROTOS, 1), jnp.float32)
    return jnp.exp(math.log(0.25) + spread * (math.log(8.0) - math.log(0.25)))


def draw_teacher_feat(key, part):
    common = shared_features(key)
    values = jnp.clip(common, -6.0, 6.0)
    return values.astype(jnp.bfloat16)


def draw_student_feat(key, part):
    common = shared_features(key)
    key = jax.random.fold_in(key, 12)
    private = jax.random.normal(jax.random.fold_in(key, 1), (ROWS, D), jnp.float32)
    values = jnp.clip(0.8 * common + 0.6 * private, -6.0, 6.0)
    return values.astype(jnp.bfloat16)


def draw_teacher_proto(key, part):
    common = shared_centers(key)
    factors = proto_factors(key)
    values = jnp.clip(common, -4.0, 4.0) * factors * D ** (-0.5)
    values = jnp.clip(values, -2.0, 2.0)
    return values.astype(jnp.bfloat16)


def draw_student_proto(key, part):
    common = shared_centers(key)
    key = jax.random.fold_in(key, 14)
    private = jax.random.normal(jax.random.fold_in(key, 1), (PROTOS, D), jnp.float32)
    values = jnp.clip((0.8 * common + 0.6 * private) * D ** (-0.5), -0.375, 0.375)
    return values.astype(jnp.bfloat16)


def setup_inputs(seed: int = 0) -> dict:
    key_list = jax.random.split(jax.random.key(seed), 5)
    teacher_feat = draw_teacher_feat(jax.random.fold_in(key_list[4], 71), 0)
    student_feat = draw_student_feat(jax.random.fold_in(key_list[4], 71), 0)
    teacher_proto = draw_teacher_proto(jax.random.fold_in(key_list[4], 71), 0)
    student_proto = draw_student_proto(jax.random.fold_in(key_list[4], 71), 0)
    return {"teacher_feat": teacher_feat, "student_feat": student_feat, "teacher_proto": teacher_proto, "student_proto": student_proto}


teacher_temp = 0.07
student_temp = 0.1


def logit_tiles(embedding_lines, center_table, sharpening_divisor):
    block_cols = min(8192, PROTOS)
    coefficient_table = center_table.astype(jnp.float32).reshape(PROTOS // block_cols, block_cols, D)
    given_tensors = embedding_lines.astype(jnp.float32)
    return lax.map(lambda tile_window: jnp.dot(given_tensors, tile_window.T, precision=lax.Precision.HIGHEST) / sharpening_divisor, coefficient_table)


def reference(teacher_feat, student_feat, teacher_proto, student_proto):
    teacher_scores = logit_tiles(teacher_feat, teacher_proto, teacher_temp)
    colmax = jnp.max(teacher_scores, axis=1)
    weight_rows = jnp.ones((ROWS,), jnp.float32)
    col_scale = jnp.ones_like(colmax)
    for sweep_step in range(ITERS):
        colsum = lax.map(lambda pair: jnp.dot(weight_rows, jnp.exp(pair[0] - pair[1][None, :]), precision=lax.Precision.HIGHEST), (teacher_scores, colmax))
        col_scale = 1.0 / (PROTOS * colsum)

        def add_rows(summed, triple):
            return summed + jnp.dot(jnp.exp(triple[0] - triple[1][None, :]), triple[2], precision=lax.Precision.HIGHEST), None

        rowsum, unused = lax.scan(add_rows, jnp.zeros((ROWS,), jnp.float32), (teacher_scores, colmax, col_scale))
        weight_rows = 1.0 / (ROWS * rowsum)
    logits = logit_tiles(student_feat, student_proto, student_temp)
    logit_max = jnp.max(logits, axis=(0, 2))
    logit_sum = jnp.sum(lax.map(lambda tile_window: jnp.sum(jnp.exp(tile_window - logit_max[:, None]), axis=1), logits), axis=0)
    log_norm = logit_max + jnp.log(logit_sum)
    block_count = logits.shape[0]
    student_blocks = student_proto.astype(jnp.float32).reshape(block_count, PROTOS // block_count, D)

    def finish(carried, pieces):
        grad_sum, loss_sum = carried
        scores, col_top, col_factor, logit_block, coefficient_table = pieces
        plan = ROWS * weight_rows[:, None] * jnp.exp(scores - col_top[None, :]) * col_factor[None, :]
        log_probs = logit_block - log_norm[:, None]
        loss_sum = loss_sum - jnp.sum(plan * log_probs)
        logit_grad = ((jnp.exp(log_probs) - plan) / (ROWS * student_temp)).astype(jnp.bfloat16)
        grad_sum = grad_sum + jnp.dot(logit_grad.astype(jnp.float32), coefficient_table, precision=lax.Precision.HIGHEST)
        return (grad_sum, loss_sum), plan.astype(jnp.bfloat16)

    init = (jnp.zeros((ROWS, D), jnp.float32), jnp.zeros((), jnp.float32))
    (feature_grad, loss_value), target_blocks = lax.scan(finish, init, (teacher_scores, colmax, col_scale, logits, student_blocks))
    targets = jnp.transpose(target_blocks, (1, 0, 2)).reshape(ROWS, PROTOS)
    return (targets, feature_grad, loss_value / ROWS)
```

```python
import jax
import jax.numpy as jnp
from jax import lax
from jax.experimental import pallas as pl
from jax.experimental.pallas import tpu as pltpu
from jax.sharding import PartitionSpec as P

PROTOS = 131072
ROWS = 4096
TEACHER_TEMP = 0.07
STUDENT_TEMP = 0.1
LOG2E = 1.4426950408889634
KT = LOG2E / TEACHER_TEMP
KS = LOG2E / STUDENT_TEMP
F32 = jnp.float32
BF16 = jnp.bfloat16
NT = (((1,), (1,)), ((), ()))
Z_ORDER = (8, 7, 9, 6, 10, 5, 11, 4, 12, 3, 13, 2, 14, 1, 15)


def across(row):
    return jnp.broadcast_to(row, (128, 128)).T


def lane_sums(a):
    return jnp.sum(a.T, axis=0, keepdims=True)


def twice(a):
    return jnp.concatenate([a, a], axis=1)


def halves(a):
    return a[:, :128] + a[:, 128:]


def product(values, centers):
    high = values.astype(BF16)
    low = (values - high.astype(F32)).astype(BF16)
    return jnp.dot(high, centers, preferred_element_type=F32) + jnp.dot(
        low, centers, preferred_element_type=F32
    )


def kernel(
    tf, sf, tp, sp,
    targets, grad, loss,
    TF, SF, TP, SP, K2, KR, LG, TG,
    MC, CS, FS, CE, ACC, WB,
    C1, CB, RY, RZ, MY, CY, ST, BS, BR, RT, AS, AR, GS, LY, LC,
    local_sem, gather_send, gather_recv, ex_send, ex_recv, out_sem,
):
    b, z = lax.axis_index("batch"), lax.axis_index("proto")
    y, x, c = b // 8, lax.rem(b // 2, 4), lax.rem(b, 2)
    xc = lax.rem(b, 8)

    def at(y_, x_, c_):
        return {"batch": (lax.rem(y_, 4) * 4 + lax.rem(x_, 4)) * 2 + c_}

    sibling = at(y, x, 1 - c)
    y_group = [at(y + i, x, c) for i in (1, 3, 2)]
    xc_group = [{"batch": y * 8 + lax.rem(xc + i, 8)} for i in range(1, 8)]
    z_group = [{"proto": lax.rem(z + i, 16)} for i in Z_ORDER]

    loads = [
        pltpu.make_async_copy(tp, TP.at[c, y, x], local_sem.at[0]),
        pltpu.make_async_copy(tf, TF.at[y], local_sem.at[1]),
        pltpu.make_async_copy(sp, SP.at[c, x, y], local_sem.at[2]),
        pltpu.make_async_copy(sf, SF, local_sem.at[3]),
    ]
    for load in loads:
        load.start()

    barrier = pltpu.get_barrier_semaphore()
    partners = z_group + xc_group + y_group
    for partner in partners:
        pl.semaphore_signal(barrier, inc=1, device_id=partner)
    pl.semaphore_wait(barrier, len(partners))

    unsent = []
    used = [0]

    def send(ref, device, recv_sem, dst=None):
        k = used[0]
        used[0] += 1
        copy = pltpu.make_async_remote_copy(
            src_ref=ref,
            dst_ref=ref if dst is None else dst,
            send_sem=gather_send.at[k],
            recv_sem=recv_sem,
            device_id=device,
        )
        copy.start()
        unsent.append((ref, gather_send.at[k]))

    def arrived(ref, sem):
        pltpu.make_async_copy(ref, ref, sem).wait()

    exchanges = [0]

    def exchange(buf, me, group):
        k = exchanges[0]
        exchanges[0] += 1
        for device in group:
            pltpu.make_async_remote_copy(
                src_ref=buf.at[me],
                dst_ref=buf.at[me],
                send_sem=ex_send.at[k],
                recv_sem=ex_recv.at[k],
                device_id=device,
            ).start()
        all_of = buf.at[pl.ds(0, len(group))]
        unsent.append((all_of, ex_send.at[k]))
        return lambda: arrived(all_of, ex_recv.at[k])

    def scatter(src, buf):
        k = exchanges[0]
        exchanges[0] += 1
        for i in Z_ORDER:
            t = lax.rem(z + i, 16)
            pltpu.make_async_remote_copy(
                src_ref=src.at[t],
                dst_ref=buf.at[z],
                send_sem=ex_send.at[k],
                recv_sem=ex_recv.at[k],
                device_id={"proto": t},
            ).start()
        buf[z] = src[z]
        all_of = buf.at[pl.ds(0, 15)]
        unsent.append((all_of, ex_send.at[k]))
        return lambda: arrived(all_of, ex_recv.at[k])

    loads[0].wait()
    for i in (1, 3, 2):
        send(TP.at[c, y, x], at(y, x + i, c), gather_recv.at[i - 1])
    send(TP.at[c, y, x], sibling, gather_recv.at[3])
    loads[1].wait()
    for i in (1, 3, 2):
        send(TF.at[y], at(y + i, x, c), gather_recv.at[6 + i])
    loads[2].wait()
    for i in (1, 3, 2):
        send(SP.at[c, x, y], at(y + i, x, c), gather_recv.at[9 + i])
    loads[3].wait()

    for i in (1, 3, 2):
        block = TP.at[c, y, lax.rem(x + 4 - i, 4)]
        arrived(block, gather_recv.at[i - 1])
        send(block, sibling, gather_recv.at[3 + i])
    for i in (1, 3, 2):
        send(TP.at[c, y], at(y + i, x, c), gather_recv.at[12 + i])
    for i in (1, 3, 2):
        arrived(TF.at[lax.rem(y + 4 - i, 4)], gather_recv.at[6 + i])

    def score_block(cc, xx):
        j = cc * 4 + xx
        scores = lax.dot_general(
            TF[...].reshape(512, 256), TP[cc, y, xx], NT, preferred_element_type=F32
        )
        K2[j] = scores
        top = jnp.max(scores, axis=0, keepdims=True)
        MC[pl.ds(j, 1), :] = top
        total = jnp.zeros((1, 256), F32)
        for q in range(4):
            e = jnp.exp2((K2[j, q * 128 : q * 128 + 128, :] - top) * KT)
            K2[j, q * 128 : q * 128 + 128, :] = e
            total = total + jnp.sum(e, axis=0, keepdims=True)
        CS[pl.ds(j, 1), :] = total

    @pl.loop(0, 4)
    def _(xx):
        score_block(c, xx)

    for i in range(4):
        arrived(TP.at[1 - c, y, lax.rem(x + 4 - i, 4)], gather_recv.at[3 + i])

    @pl.loop(0, 4)
    def _(xx):
        score_block(1 - c, xx)

    C1[xc, 0] = MC[...]
    C1[xc, 1] = CS[...]
    wait_c1 = exchange(C1, xc, xc_group)
    for i in (1, 3, 2):
        arrived(SP.at[c, x, lax.rem(y + 4 - i, 4)], gather_recv.at[9 + i])
    for i in (1, 3, 2):
        send(SP.at[c, x], at(y, x + i, c), gather_recv.at[15 + i])
    wait_c1()
    top = C1[0, 0]
    for d in range(1, 8):
        top = jnp.maximum(top, C1[d, 0])
    total = jnp.zeros((8, 256), F32)
    for d in range(8):
        total = total + C1[d, 1] * jnp.exp2((C1[d, 0] - top) * KT)
    FS[...] = jnp.exp2((MC[...] - top) * KT)
    MY[y] = top
    wait_my = exchange(MY, y, y_group)
    CE[...] = FS[...] / (PROTOS * total)

    def row_pass(it):
        @pl.loop(0, 8)
        def _(q):
            rows = pl.ds(pl.multiple_of(q * 64, 64), 64)
            acc = jnp.zeros((64, 128), F32)
            for j in range(8):
                acc = acc + halves(K2[j, rows, :] * CE[j : j + 1, :])
            ACC[rows, :] = acc

        for q in range(4):
            RY[it, y, q : q + 1, :] = lane_sums(ACC[q * 128 : q * 128 + 128, :])
        exchange(RY.at[it], y, y_group)()
        r = RY[it, 0]
        for d in range(1, 4):
            r = r + RY[it, d]
        RZ[it, z] = r
        return exchange(RZ.at[it], z, z_group)

    def row_end(it, wait):
        wait()
        r = RZ[it, 0]
        for d in range(1, 16):
            r = r + RZ[it, d]
        w = 1.0 / (ROWS * r)
        for q in range(4):
            WB[q] = across(w[q : q + 1, :])

    def col_pass(it):
        @pl.loop(0, 8)
        def _(j):
            total = jnp.zeros((1, 256), F32)
            for q in range(4):
                part = K2[j, q * 128 : q * 128 + 128, :] * twice(WB[q])
                total = total + jnp.sum(part, axis=0, keepdims=True)
            CS[pl.ds(j, 1), :] = total

        CB[it, xc] = CS[...] * FS[...]
        return exchange(CB.at[it], xc, xc_group)

    def col_end(it, wait):
        wait()
        total = CB[it, 0]
        for d in range(1, 8):
            total = total + CB[it, d]
        return 1.0 / (PROTOS * total)

    wait_row = row_pass(0)
    row_end(0, wait_row)
    col = col_end(0, col_pass(0))
    CE[...] = col * FS[...]
    wait_row = row_pass(1)

    for i in (1, 3, 2):
        part = TP.at[c, lax.rem(y + 4 - i, 4)]
        arrived(part, gather_recv.at[12 + i])
        send(part, sibling, gather_recv.at[18 + i])
    send(SP.at[c, x], sibling, gather_recv.at[22])
    for i in (1, 3, 2):
        part = SP.at[c, lax.rem(x + 4 - i, 4)]
        arrived(part, gather_recv.at[15 + i])
        send(part, sibling, gather_recv.at[22 + i])
    wait_my()

    for i in (1, 3, 2):
        arrived(TP.at[1 - c, lax.rem(y + 4 - i, 4)], gather_recv.at[18 + i])

    def place(g):
        return g // 8, lax.rem(g // 2, 4), lax.rem(g, 2)

    @pl.loop(0, 32)
    def _(g):
        yy, xx, cc = place(g)
        scores = lax.dot_general(TF[y], TP[cc, yy, xx], NT, preferred_element_type=F32)
        KR[g] = jnp.exp2((scores - MY[yy, pl.ds(cc * 4 + xx, 1), :]) * KT)

    row_end(1, wait_row)
    wait_col = col_pass(1)

    for i in range(4):
        arrived(SP.at[1 - c, lax.rem(x + 4 - i, 4)], gather_recv.at[22 + i])

    def logit_block(g, most):
        yy, xx, cc = place(g)
        logits = lax.dot_general(SF[...], SP[cc, xx, yy], NT, preferred_element_type=F32)
        LG[g] = logits
        return jnp.maximum(most, jnp.maximum(logits[:, :128], logits[:, 128:]))

    most = lax.fori_loop(0, 32, logit_block, jnp.full((128, 128), -jnp.inf, F32))
    most = jnp.max(most, axis=1, keepdims=True)

    def softmax_block(g, carried):
        total, out = carried
        yy, xx, cc = place(g)
        below = LG[g] - most
        LG[g] = below
        e = jnp.exp2(below * KS)
        return total + halves(e), out + product(e, SP[cc, xx, yy])

    total, soft = lax.fori_loop(
        0, 32, softmax_block, (jnp.zeros((128, 128), F32), jnp.zeros((128, 256), F32))
    )
    ST[z, 0:1, :] = jnp.broadcast_to(most, (128, 128)).T[0:1, :]
    ST[z, 1:2, :] = lane_sums(total)
    wait_st = exchange(ST, z, z_group)

    CY[y] = col_end(1, wait_col)
    wait_cy = exchange(CY, y, y_group)

    wait_st()
    tops = ST[:, 0, :]
    row_top = jnp.max(tops, axis=0, keepdims=True)
    row_sum = jnp.sum(ST[:, 1, :] * jnp.exp2((tops - row_top) * KS), axis=0, keepdims=True)
    below_top = ST[z, 0:1, :] - row_top
    BS[...] = (soft * twice(across(jnp.exp2(below_top * KS) / row_sum))).reshape(16, 8, 256)
    wait_b = scatter(BS, BR)
    wait_cy()

    def plan_block(g, carried):
        rsum, tsum, out = carried
        yy, xx, cc = place(g)
        share = KR[g] * CY[yy, pl.ds(cc * 4 + xx, 1), :]
        KR[g] = share
        return (
            rsum + halves(share),
            tsum + halves(share * LG[g]),
            out + product(share, SP[cc, xx, yy]),
        )

    rsum, tsum, out = lax.fori_loop(
        0,
        32,
        plan_block,
        (jnp.zeros((128, 128), F32), jnp.zeros((128, 128), F32), jnp.zeros((128, 256), F32)),
    )
    r = lane_sums(rsum)
    RT[z, 0:1, :] = r
    RT[z, 1:2, :] = lane_sums(tsum) + r * below_top
    wait_rt = exchange(RT, z, z_group)
    AS[...] = out.reshape(16, 8, 256)
    wait_a = scatter(AS, AR)

    wait_rt()
    r, t = RT[0, 0:1, :], RT[0, 1:2, :]
    for d in range(1, 16):
        r, t = r + RT[d, 0:1, :], t + RT[d, 1:2, :]
    weight = 1.0 / r
    part = jnp.log(row_sum) - weight * t * (1.0 / STUDENT_TEMP)
    LY[y] = jnp.broadcast_to(part, (8, 128))
    wait_ly = exchange(LY, y, y_group)
    WB[0] = across(weight)

    wait_b()
    wait_a()
    plan_sum, soft_sum = AR[0], BR[0]
    for d in range(1, 16):
        plan_sum, soft_sum = plan_sum + AR[d], soft_sum + BR[d]
    mine = WB[0, pl.ds(pl.multiple_of(z * 8, 8), 8), :]
    GS[z] = (soft_sum - twice(mine) * plan_sum) / (ROWS * STUDENT_TEMP)
    wait_gs = exchange(GS, z, z_group)

    writes = []
    for q in range(4):

        @pl.loop(0, 8)
        def _(n):
            g = q * 8 + n
            columns = pl.ds(pl.multiple_of(g * 256, 256), 256)
            TG[:, columns] = (KR[g] * twice(WB[0])).astype(BF16)

        columns = slice(q * 2048, q * 2048 + 2048)
        write = pltpu.make_async_copy(TG.at[:, columns], targets.at[:, columns], out_sem.at[q])
        write.start()
        writes.append(write)

    wait_ly()
    LC[xc] = ((LY[0] + LY[1]) + LY[2]) + LY[3]
    wait_lc = exchange(LC, xc, xc_group)
    wait_lc()
    part = LC[0]
    for d in range(1, 8):
        part = part + LC[d]
    loss[...] = jnp.sum(part, axis=1, keepdims=True)[0:1, :] / ROWS

    wait_gs()
    grad[...] = GS[...].reshape(128, 256)
    for write in writes:
        write.wait()
    for ref, sem in unsent:
        arrived(ref, sem)


def on_device(teacher_feat, student_feat, teacher_proto, student_proto):
    any_spec = pl.BlockSpec(memory_space=pl.ANY)
    vmem_spec = pl.BlockSpec(memory_space=pltpu.VMEM)

    def f32(*shape):
        return pltpu.VMEM(shape, F32)

    def bf16(*shape):
        return pltpu.VMEM(shape, BF16)

    targets, grad, loss = pl.pallas_call(
        kernel,
        out_shape=(
            jax.ShapeDtypeStruct((128, 8192), BF16),
            jax.ShapeDtypeStruct((128, 256), F32),
            jax.ShapeDtypeStruct((1, 1), F32),
        ),
        in_specs=[any_spec] * 4,
        out_specs=(any_spec, vmem_spec, vmem_spec),
        scratch_shapes=[
            bf16(4, 128, 256),
            bf16(128, 256),
            bf16(2, 4, 4, 256, 256),
            bf16(2, 4, 4, 256, 256),
            f32(8, 512, 256),
            f32(32, 128, 256),
            f32(32, 128, 256),
            bf16(128, 8192),
            f32(8, 256),
            f32(8, 256),
            f32(8, 256),
            f32(8, 256),
            f32(512, 128),
            f32(4, 128, 128),
            f32(8, 2, 8, 256),
            f32(2, 8, 8, 256),
            f32(2, 4, 4, 128),
            f32(2, 16, 4, 128),
            f32(4, 8, 256),
            f32(4, 8, 256),
            f32(16, 2, 128),
            f32(16, 8, 256),
            f32(16, 8, 256),
            f32(16, 2, 128),
            f32(16, 8, 256),
            f32(16, 8, 256),
            f32(16, 8, 256),
            f32(4, 8, 128),
            f32(8, 8, 128),
            pltpu.SemaphoreType.DMA((4,)),
            pltpu.SemaphoreType.DMA((26,)),
            pltpu.SemaphoreType.DMA((26,)),
            pltpu.SemaphoreType.DMA((16,)),
            pltpu.SemaphoreType.DMA((16,)),
            pltpu.SemaphoreType.DMA((4,)),
        ],
        compiler_params=pltpu.CompilerParams(
            collective_id=0, has_side_effects=True, vmem_limit_bytes=48 * 2**20
        ),
        cost_estimate=pl.CostEstimate(
            flops=2_000_000_000, bytes_accessed=4_000_000, transcendentals=4_000_000
        ),
    )(teacher_feat, student_feat, teacher_proto, student_proto)
    return targets, grad, loss[0, 0]


def solution(mesh):
    return jax.shard_map(
        on_device,
        mesh=mesh,
        in_specs=(
            P("batch", None),
            P("batch", None),
            P(("proto", "batch"), None),
            P(("proto", "batch"), None),
        ),
        out_specs=(P("batch", "proto"), P("batch", None), P()),
        check_vma=False,
    )
```

```python
import jax
import jax.numpy as jnp
from jax import lax
from jax.experimental import pallas as pl
from jax.experimental.pallas import tpu as pltpu
from jax.sharding import PartitionSpec as P

PROTOS = 131072
ROWS = 4096
TEACHER_TEMP = 0.07
STUDENT_TEMP = 0.1
LOG2E = 1.4426950408889634
KT = LOG2E / TEACHER_TEMP
KS = LOG2E / STUDENT_TEMP
F32 = jnp.float32
BF16 = jnp.bfloat16
NT = (((1,), (1,)), ((), ()))
Z_ORDER = (8, 7, 9, 6, 10, 5, 11, 4, 12, 3, 13, 2, 14, 1, 15)


def across(row):
    return jnp.broadcast_to(row, (128, 128)).T


def lane_sums(a):
    return jnp.sum(a.T, axis=0, keepdims=True)


def twice(a):
    return jnp.concatenate([a, a], axis=1)


def halves(a):
    return a[:, :128] + a[:, 128:]


def product(values, centers):
    high = values.astype(BF16)
    low = (values - high.astype(F32)).astype(BF16)
    return jnp.dot(high, centers, preferred_element_type=F32) + jnp.dot(
        low, centers, preferred_element_type=F32
    )


def kernel(
    tf, sf, tp, sp,
    targets, grad, loss,
    TF, SF, TP, SP, K2, KR, LG, TG,
    MC, CS, FS, CE, ACC, WB, TOPS, SUMS, SOFT,
    C1, CB, RY, RZ, MY, CY, ST, BS, BR, RT, AS, AR, GS, LY, LC,
    local_sem, gather_send, gather_recv, ex_send, ex_recv, out_sem,
):
    b, z = lax.axis_index("batch"), lax.axis_index("proto")
    y, x, c = b // 8, lax.rem(b // 2, 4), lax.rem(b, 2)
    xc = lax.rem(b, 8)

    def at(y_, x_, c_):
        return {"batch": (lax.rem(y_, 4) * 4 + lax.rem(x_, 4)) * 2 + c_}

    sibling = at(y, x, 1 - c)
    y_group = [at(y + i, x, c) for i in (1, 3, 2)]
    xc_group = [{"batch": y * 8 + lax.rem(xc + i, 8)} for i in range(1, 8)]
    z_group = [{"proto": lax.rem(z + i, 16)} for i in Z_ORDER]

    loads = [
        pltpu.make_async_copy(tp, TP.at[c, y, x], local_sem.at[0]),
        pltpu.make_async_copy(tf, TF.at[y], local_sem.at[1]),
        pltpu.make_async_copy(sp, SP.at[c, x, y], local_sem.at[2]),
        pltpu.make_async_copy(sf, SF, local_sem.at[3]),
    ]
    for load in loads:
        load.start()

    barrier = pltpu.get_barrier_semaphore()
    partners = z_group + xc_group + y_group
    for partner in partners:
        pl.semaphore_signal(barrier, inc=1, device_id=partner)
    pl.semaphore_wait(barrier, len(partners))

    unsent = []
    used = [0]

    def send(ref, device, recv_sem, dst=None):
        k = used[0]
        used[0] += 1
        copy = pltpu.make_async_remote_copy(
            src_ref=ref,
            dst_ref=ref if dst is None else dst,
            send_sem=gather_send.at[k],
            recv_sem=recv_sem,
            device_id=device,
        )
        copy.start()
        unsent.append((ref, gather_send.at[k]))

    def arrived(ref, sem):
        pltpu.make_async_copy(ref, ref, sem).wait()

    exchanges = [0]

    def exchange(buf, me, group):
        k = exchanges[0]
        exchanges[0] += 1
        for device in group:
            pltpu.make_async_remote_copy(
                src_ref=buf.at[me],
                dst_ref=buf.at[me],
                send_sem=ex_send.at[k],
                recv_sem=ex_recv.at[k],
                device_id=device,
            ).start()
        all_of = buf.at[pl.ds(0, len(group))]
        unsent.append((all_of, ex_send.at[k]))
        return lambda: arrived(all_of, ex_recv.at[k])

    def scatter(src, buf):
        k = exchanges[0]
        exchanges[0] += 1
        for i in Z_ORDER:
            t = lax.rem(z + i, 16)
            pltpu.make_async_remote_copy(
                src_ref=src.at[t],
                dst_ref=buf.at[z],
                send_sem=ex_send.at[k],
                recv_sem=ex_recv.at[k],
                device_id={"proto": t},
            ).start()
        buf[z] = src[z]
        all_of = buf.at[pl.ds(0, 15)]
        unsent.append((all_of, ex_send.at[k]))
        return lambda: arrived(all_of, ex_recv.at[k])

    loads[0].wait()
    for i in (1, 3, 2):
        send(TP.at[c, y, x], at(y, x + i, c), gather_recv.at[i - 1])
    send(TP.at[c, y, x], sibling, gather_recv.at[3])
    loads[1].wait()
    for i in (1, 3, 2):
        send(TF.at[y], at(y + i, x, c), gather_recv.at[6 + i])
    loads[2].wait()
    for i in (1, 3, 2):
        send(SP.at[c, x, y], at(y + i, x, c), gather_recv.at[9 + i])
    loads[3].wait()

    for i in (1, 3, 2):
        block = TP.at[c, y, lax.rem(x + 4 - i, 4)]
        arrived(block, gather_recv.at[i - 1])
        send(block, sibling, gather_recv.at[3 + i])
    for i in (1, 3, 2):
        arrived(TF.at[lax.rem(y + 4 - i, 4)], gather_recv.at[6 + i])

    def score_block(cc, xx):
        j = cc * 4 + xx
        scores = lax.dot_general(
            TF[...].reshape(512, 256), TP[cc, y, xx], NT, preferred_element_type=F32
        )
        K2[j] = scores
        top = jnp.max(scores, axis=0, keepdims=True)
        MC[pl.ds(j, 1), :] = top
        total = jnp.zeros((1, 256), F32)
        for q in range(4):
            e = jnp.exp2((K2[j, q * 128 : q * 128 + 128, :] - top) * KT)
            K2[j, q * 128 : q * 128 + 128, :] = e
            total = total + jnp.sum(e, axis=0, keepdims=True)
        CS[pl.ds(j, 1), :] = total

    @pl.loop(0, 4)
    def _(xx):
        score_block(c, xx)

    for i in range(4):
        arrived(TP.at[1 - c, y, lax.rem(x + 4 - i, 4)], gather_recv.at[3 + i])

    @pl.loop(0, 4)
    def _(xx):
        score_block(1 - c, xx)

    C1[xc, 0] = MC[...]
    C1[xc, 1] = CS[...]
    wait_c1 = exchange(C1, xc, xc_group)
    for i in (1, 3, 2):
        arrived(SP.at[c, x, lax.rem(y + 4 - i, 4)], gather_recv.at[9 + i])
    wait_c1()
    send(SP.at[c, x, pl.ds(0, 3)], at(y, x + 1, c), gather_recv.at[13])
    send(SP.at[c, x, pl.ds(0, 3)], at(y, x + 3, c), gather_recv.at[14])
    send(SP.at[c, x], sibling, gather_recv.at[15])
    top = C1[0, 0]
    for d in range(1, 8):
        top = jnp.maximum(top, C1[d, 0])
    total = jnp.zeros((8, 256), F32)
    for d in range(8):
        total = total + C1[d, 1] * jnp.exp2((C1[d, 0] - top) * KT)
    FS[...] = jnp.exp2((MC[...] - top) * KT)
    MY[y] = top
    wait_my = exchange(MY, y, y_group)
    CE[...] = FS[...] / (PROTOS * total)

    def row_pass(it):
        @pl.loop(0, 8)
        def _(q):
            rows = pl.ds(pl.multiple_of(q * 64, 64), 64)
            acc = jnp.zeros((64, 128), F32)
            for j in range(8):
                acc = acc + halves(K2[j, rows, :] * CE[j : j + 1, :])
            ACC[rows, :] = acc

        for q in range(4):
            RY[it, y, q : q + 1, :] = lane_sums(ACC[q * 128 : q * 128 + 128, :])
        exchange(RY.at[it], y, y_group)()
        r = RY[it, 0]
        for d in range(1, 4):
            r = r + RY[it, d]
        RZ[it, z] = r
        return exchange(RZ.at[it], z, z_group)

    def row_end(it, wait):
        wait()
        r = RZ[it, 0]
        for d in range(1, 16):
            r = r + RZ[it, d]
        w = 1.0 / (ROWS * r)
        for q in range(4):
            WB[q] = across(w[q : q + 1, :])

    def col_pass(it):
        @pl.loop(0, 8)
        def _(j):
            total = jnp.zeros((1, 256), F32)
            for q in range(4):
                part = K2[j, q * 128 : q * 128 + 128, :] * twice(WB[q])
                total = total + jnp.sum(part, axis=0, keepdims=True)
            CS[pl.ds(j, 1), :] = total

        CB[it, xc] = CS[...] * FS[...]
        return exchange(CB.at[it], xc, xc_group)

    def col_end(it, wait):
        wait()
        total = CB[it, 0]
        for d in range(1, 8):
            total = total + CB[it, d]
        return 1.0 / (PROTOS * total)

    x_less, x_more, x_far = lax.rem(x + 3, 4), lax.rem(x + 1, 4), lax.rem(x + 2, 4)
    y_less, y_more, y_far = lax.rem(y + 3, 4), lax.rem(y + 1, 4), lax.rem(y + 2, 4)
    low, high = pl.ds(0, 2), pl.ds(2, 2)

    def kernel_rows(yy):
        @pl.loop(0, 8)
        def _(j):
            cc, xx = j // 4, lax.rem(j, 4)
            scores = lax.dot_general(TF[y], TP[cc, yy, xx], NT, preferred_element_type=F32)
            KR[(yy * 4 + xx) * 2 + cc] = jnp.exp2((scores - MY[yy, pl.ds(j, 1), :]) * KT)

    def softmax_part(xs):
        old = TOPS[...]
        top = old
        for xx in xs:

            def logit_block(n, top, xx=xx):
                cc, yy = n // 4, lax.rem(n, 4)
                logits = lax.dot_general(SF[...], SP[cc, xx, yy], NT, preferred_element_type=F32)
                LG[(yy * 4 + xx) * 2 + cc] = logits
                return jnp.maximum(top, jnp.maximum(logits[:, :128], logits[:, 128:]))

            top = lax.fori_loop(0, 8, logit_block, top)
        top = jnp.broadcast_to(jnp.max(top, axis=1, keepdims=True), (128, 128))
        shrink = jnp.exp2((old - top) * KS)
        TOPS[...] = top
        state = SUMS[...] * shrink, SOFT[...] * twice(shrink)
        for xx in xs:

            def softmax_block(n, carried, xx=xx):
                total, out = carried
                cc, yy = n // 4, lax.rem(n, 4)
                e = jnp.exp2((LG[(yy * 4 + xx) * 2 + cc] - twice(TOPS[...])) * KS)
                return total + halves(e), out + product(e, SP[cc, xx, yy])

            state = lax.fori_loop(0, 8, softmax_block, state)
        SUMS[...], SOFT[...] = state

    TOPS[...] = jnp.full((128, 128), -jnp.inf, F32)
    SUMS[...] = jnp.zeros((128, 128), F32)
    SOFT[...] = jnp.zeros((128, 256), F32)

    wait_row = row_pass(0)
    send(TP.at[c, y], at(y + 1, x, c), gather_recv.at[16])
    send(TP.at[c, y], at(y + 3, x, c), gather_recv.at[17])
    kernel_rows(y)
    arrived(SP.at[1 - c, x], gather_recv.at[15])
    softmax_part((x,))
    row_end(0, wait_row)
    col = col_end(0, col_pass(0))
    CE[...] = col * FS[...]
    arrived(SP.at[c, x_less, pl.ds(0, 3)], gather_recv.at[13])
    arrived(SP.at[c, x_more, pl.ds(0, 3)], gather_recv.at[14])
    send(SP.at[c, x, pl.ds(3, 1)], at(y, x + 1, c), gather_recv.at[18])
    send(SP.at[c, x, pl.ds(3, 1)], at(y, x + 3, c), gather_recv.at[19])
    send(SP.at[c, x_less, low], at(y, x + 1, c), gather_recv.at[20])
    send(SP.at[c, x_more, pl.ds(2, 1)], at(y, x + 3, c), gather_recv.at[21])
    send(SP.at[c, x_less, pl.ds(0, 3)], sibling, gather_recv.at[22])
    send(SP.at[c, x_more, pl.ds(0, 3)], sibling, gather_recv.at[23])

    wait_row = row_pass(1)
    arrived(TP.at[c, y_less], gather_recv.at[16])
    arrived(TP.at[c, y_more], gather_recv.at[17])
    send(TP.at[c, y_less, low], at(y + 1, x, c), gather_recv.at[24])
    send(TP.at[c, y_more, high], at(y + 3, x, c), gather_recv.at[25])
    arrived(SP.at[c, x_less, pl.ds(3, 1)], gather_recv.at[18])
    arrived(SP.at[c, x_more, pl.ds(3, 1)], gather_recv.at[19])
    send(SP.at[c, x_more, pl.ds(3, 1)], at(y, x + 3, c), gather_recv.at[26])
    send(SP.at[c, x_less, pl.ds(3, 1)], sibling, gather_recv.at[27])
    send(SP.at[c, x_more, pl.ds(3, 1)], sibling, gather_recv.at[28])
    send(TP.at[c, y_less], sibling, gather_recv.at[29])
    send(TP.at[c, y_more], sibling, gather_recv.at[30])
    arrived(SP.at[1 - c, x_less, pl.ds(0, 3)], gather_recv.at[22])
    arrived(SP.at[1 - c, x_more, pl.ds(0, 3)], gather_recv.at[23])
    arrived(SP.at[1 - c, x_less, pl.ds(3, 1)], gather_recv.at[27])
    arrived(SP.at[1 - c, x_more, pl.ds(3, 1)], gather_recv.at[28])
    softmax_part((x_less, x_more))
    row_end(1, wait_row)
    wait_col = col_pass(1)

    arrived(SP.at[c, x_far, low], gather_recv.at[20])
    arrived(SP.at[c, x_far, pl.ds(2, 1)], gather_recv.at[21])
    arrived(SP.at[c, x_far, pl.ds(3, 1)], gather_recv.at[26])
    send(SP.at[c, x_far], sibling, gather_recv.at[31])
    arrived(TP.at[c, y_far, low], gather_recv.at[24])
    arrived(TP.at[c, y_far, high], gather_recv.at[25])
    send(TP.at[c, y_far], sibling, gather_recv.at[32])
    wait_my()
    arrived(TP.at[1 - c, y_less], gather_recv.at[29])
    arrived(TP.at[1 - c, y_more], gather_recv.at[30])
    kernel_rows(y_less)
    kernel_rows(y_more)

    CY[y] = col_end(1, wait_col)
    wait_cy = exchange(CY, y, y_group)

    arrived(SP.at[1 - c, x_far], gather_recv.at[31])
    softmax_part((x_far,))
    ST[z, 0:1, :] = TOPS[...].T[0:1, :]
    ST[z, 1:2, :] = lane_sums(SUMS[...])
    wait_st = exchange(ST, z, z_group)
    BS[...] = SOFT[...].reshape(16, 8, 256)
    wait_b = scatter(BS, BR)
    arrived(TP.at[1 - c, y_far], gather_recv.at[32])
    kernel_rows(y_far)
    wait_cy()

    def place(g):
        return g // 8, lax.rem(g // 2, 4), lax.rem(g, 2)

    def plan_block(g, carried):
        rsum, tsum, out = carried
        yy, xx, cc = place(g)
        share = KR[g] * CY[yy, pl.ds(cc * 4 + xx, 1), :]
        KR[g] = share
        return (
            rsum + halves(share),
            tsum + halves(share * (LG[g] - twice(TOPS[...]))),
            out + product(share, SP[cc, xx, yy]),
        )

    rsum, tsum, out = lax.fori_loop(
        0,
        32,
        plan_block,
        (jnp.zeros((128, 128), F32), jnp.zeros((128, 128), F32), jnp.zeros((128, 256), F32)),
    )
    RT[z, 0:1, :] = lane_sums(rsum)
    RT[z, 1:2, :] = lane_sums(tsum)
    wait_rt = exchange(RT, z, z_group)
    AS[...] = out.reshape(16, 8, 256)
    wait_a = scatter(AS, AR)

    wait_st()
    tops = ST[:, 0, :]
    row_top = jnp.max(tops, axis=0, keepdims=True)
    below = tops - row_top
    scale = jnp.exp2(below * KS)
    row_sum = jnp.sum(ST[:, 1, :] * scale, axis=0, keepdims=True)
    WB[1, :, 0:16] = (scale / row_sum).T
    wait_rt()
    r = jnp.sum(RT[:, 0, :], axis=0, keepdims=True)
    t = jnp.sum(RT[:, 1, :] + RT[:, 0, :] * below, axis=0, keepdims=True)
    weight = 1.0 / r
    part = jnp.log(row_sum) - weight * t * (1.0 / STUDENT_TEMP)
    LY[y] = jnp.broadcast_to(part, (8, 128))
    wait_ly = exchange(LY, y, y_group)
    WB[0] = across(weight)

    mine = pl.ds(pl.multiple_of(z * 8, 8), 8)
    wait_b()
    scale = WB[1, mine, :]
    soft_sum = BR[0] * scale[:, 0:1]
    for d in range(1, 16):
        soft_sum = soft_sum + BR[d] * scale[:, d : d + 1]
    wait_a()
    plan_sum = AR[0]
    for d in range(1, 16):
        plan_sum = plan_sum + AR[d]
    mixed = (soft_sum - twice(WB[0, mine, :]) * plan_sum) / (ROWS * STUDENT_TEMP)
    GS[z] = jnp.concatenate([mixed[:, :128], mixed[:, 128:]], axis=0).astype(BF16)
    wait_gs = exchange(GS, z, z_group)

    writes = []
    for q in range(4):

        @pl.loop(0, 8)
        def _(n):
            g = q * 8 + n
            columns = pl.ds(pl.multiple_of(g * 256, 256), 256)
            TG[:, columns] = (KR[g] * twice(WB[0])).astype(BF16)

        columns = slice(q * 2048, q * 2048 + 2048)
        write = pltpu.make_async_copy(TG.at[:, columns], targets.at[:, columns], out_sem.at[q])
        write.start()
        writes.append(write)

    wait_ly()
    LC[xc] = ((LY[0] + LY[1]) + LY[2]) + LY[3]
    wait_lc = exchange(LC, xc, xc_group)
    wait_lc()
    part = LC[0]
    for d in range(1, 8):
        part = part + LC[d]
    loss[...] = jnp.sum(part, axis=1, keepdims=True)[0:1, :] / ROWS

    wait_gs()
    for d in range(16):
        rows = GS[d].astype(F32)
        grad[d * 8 : d * 8 + 8, :128] = rows[:8]
        grad[d * 8 : d * 8 + 8, 128:] = rows[8:]
    for write in writes:
        write.wait()
    for ref, sem in unsent:
        arrived(ref, sem)


def on_device(teacher_feat, student_feat, teacher_proto, student_proto):
    any_spec = pl.BlockSpec(memory_space=pl.ANY)
    vmem_spec = pl.BlockSpec(memory_space=pltpu.VMEM)

    def f32(*shape):
        return pltpu.VMEM(shape, F32)

    def bf16(*shape):
        return pltpu.VMEM(shape, BF16)

    held = [
        pltpu.with_memory_space_constraint(a, pltpu.HBM)
        for a in (teacher_feat, student_feat, teacher_proto, student_proto)
    ]
    targets, grad, loss = pl.pallas_call(
        kernel,
        out_shape=(
            jax.ShapeDtypeStruct((128, 8192), BF16),
            jax.ShapeDtypeStruct((128, 256), F32),
            jax.ShapeDtypeStruct((1, 1), F32),
        ),
        in_specs=[pl.BlockSpec(memory_space=pltpu.HBM)] * 4,
        out_specs=(any_spec, vmem_spec, vmem_spec),
        scratch_shapes=[
            bf16(4, 128, 256),
            bf16(128, 256),
            bf16(2, 4, 4, 256, 256),
            bf16(2, 4, 4, 256, 256),
            f32(8, 512, 256),
            f32(32, 128, 256),
            f32(32, 128, 256),
            bf16(128, 8192),
            f32(8, 256),
            f32(8, 256),
            f32(8, 256),
            f32(8, 256),
            f32(512, 128),
            f32(4, 128, 128),
            f32(128, 128),
            f32(128, 128),
            f32(128, 256),
            f32(8, 2, 8, 256),
            f32(2, 8, 8, 256),
            f32(2, 4, 4, 128),
            f32(2, 16, 4, 128),
            f32(4, 8, 256),
            f32(4, 8, 256),
            f32(16, 2, 128),
            f32(16, 8, 256),
            f32(16, 8, 256),
            f32(16, 2, 128),
            f32(16, 8, 256),
            f32(16, 8, 256),
            bf16(16, 16, 128),
            f32(4, 8, 128),
            f32(8, 8, 128),
            pltpu.SemaphoreType.DMA((4,)),
            pltpu.SemaphoreType.DMA((40,)),
            pltpu.SemaphoreType.DMA((40,)),
            pltpu.SemaphoreType.DMA((16,)),
            pltpu.SemaphoreType.DMA((16,)),
            pltpu.SemaphoreType.DMA((4,)),
        ],
        compiler_params=pltpu.CompilerParams(
            collective_id=0, has_side_effects=True, vmem_limit_bytes=48 * 2**20
        ),
        cost_estimate=pl.CostEstimate(
            flops=2_000_000_000, bytes_accessed=4_000_000, transcendentals=4_000_000
        ),
    )(*held)
    return targets, grad, loss.reshape(())


def solution(mesh):
    return jax.shard_map(
        on_device,
        mesh=mesh,
        in_specs=(
            P("batch", None),
            P("batch", None),
            P(("proto", "batch"), None),
            P(("proto", "batch"), None),
        ),
        out_specs=(P("batch", "proto"), P("batch", None), P()),
        check_vma=False,
    )
```

```python
import jax
import jax.numpy as jnp
from jax import lax
from jax.experimental import pallas as pl
from jax.experimental.pallas import tpu as pltpu
from jax.sharding import PartitionSpec as P

PROTOS = 131072
ROWS = 4096
TEACHER_TEMP = 0.07
STUDENT_TEMP = 0.1
LOG2E = 1.4426950408889634
KT = LOG2E / TEACHER_TEMP
KS = LOG2E / STUDENT_TEMP
F32 = jnp.float32
BF16 = jnp.bfloat16
NT = (((1,), (1,)), ((), ()))
Z_ORDER = (8, 7, 9, 6, 10, 5, 11, 4, 12, 3, 13, 2, 14, 1, 15)


def across(row):
    return jnp.broadcast_to(row, (128, 128)).T


def lane_sums(a):
    return jnp.sum(a.T, axis=0, keepdims=True)


def twice(a):
    return jnp.concatenate([a, a], axis=1)


def halves(a):
    return a[:, :128] + a[:, 128:]


def product(values, centers):
    high = values.astype(BF16)
    low = (values - high.astype(F32)).astype(BF16)
    return jnp.dot(high, centers, preferred_element_type=F32) + jnp.dot(
        low, centers, preferred_element_type=F32
    )


def kernel(
    tf, sf, tp, sp,
    targets, grad, loss,
    TF, SF, TP, SP, K2, KR, LG, TG,
    MC, CS, FS, CE, ACC, WB, TOPS, SUMS, SOFT,
    C1, CB, RY, RZ, MY, CY, ST, BS, BR, RT, AS, AR, GS, LY, LC,
    relay_sem, local_sem, gather_send, gather_recv, ex_send, ex_recv, out_sem,
):
    b, z = lax.axis_index("batch"), lax.axis_index("proto")
    y, x, c = b // 8, lax.rem(b // 2, 4), lax.rem(b, 2)
    xc = lax.rem(b, 8)

    def at(y_, x_, c_):
        return {"batch": (lax.rem(y_, 4) * 4 + lax.rem(x_, 4)) * 2 + c_}

    def around(i):
        return {"proto": lax.rem(z + i, 16)}

    sibling = at(y, x, 1 - c)
    y_group = [at(y + i, x, c) for i in (1, 3, 2)]
    xc_group = [{"batch": y * 8 + lax.rem(xc + i, 8)} for i in range(1, 8)]
    z_group = [around(i) for i in Z_ORDER]

    loads = [
        pltpu.make_async_copy(tp, TP.at[c, y, x], local_sem.at[0]),
        pltpu.make_async_copy(tf, TF.at[y], local_sem.at[1]),
        pltpu.make_async_copy(sp, SP.at[c, y, x], local_sem.at[2]),
        pltpu.make_async_copy(sf, SF, local_sem.at[3]),
    ]
    for load in loads:
        load.start()

    barrier = pltpu.get_barrier_semaphore()
    partners = [around(1), around(15)] + xc_group + y_group
    for partner in partners:
        pl.semaphore_signal(barrier, inc=1, device_id=partner)
    pl.semaphore_wait(barrier, len(partners))

    def announce(k, i):
        for step in (i, 16 - i):
            pl.semaphore_signal(relay_sem.at[k], inc=1, device_id=around(step))

    announce(0, 1)

    unsent = []
    used = [0]

    def send(ref, device, recv_sem, dst=None):
        k = used[0]
        used[0] += 1
        copy = pltpu.make_async_remote_copy(
            src_ref=ref,
            dst_ref=ref if dst is None else dst,
            send_sem=gather_send.at[k],
            recv_sem=recv_sem,
            device_id=device,
        )
        copy.start()
        unsent.append((ref, gather_send.at[k]))

    def arrived(ref, sem):
        pltpu.make_async_copy(ref, ref, sem).wait()

    exchanges = [0]

    def exchange(buf, me, group):
        k = exchanges[0]
        exchanges[0] += 1
        for device in group:
            pltpu.make_async_remote_copy(
                src_ref=buf.at[me],
                dst_ref=buf.at[me],
                send_sem=ex_send.at[k],
                recv_sem=ex_recv.at[k],
                device_id=device,
            ).start()
        all_of = buf.at[pl.ds(0, len(group))]
        unsent.append((all_of, ex_send.at[k]))
        return lambda: arrived(all_of, ex_recv.at[k])

    def scatter(src, buf):
        k = exchanges[0]
        exchanges[0] += 1
        for i in Z_ORDER:
            t = lax.rem(z + i, 16)
            pltpu.make_async_remote_copy(
                src_ref=src.at[t],
                dst_ref=buf.at[z],
                send_sem=ex_send.at[k],
                recv_sem=ex_recv.at[k],
                device_id={"proto": t},
            ).start()
        buf[z] = src[z]
        all_of = buf.at[pl.ds(0, 15)]
        unsent.append((all_of, ex_send.at[k]))
        return lambda: arrived(all_of, ex_recv.at[k])

    x_less, x_more = lax.rem(x + 3, 4), lax.rem(x + 1, 4)
    y_less, y_more, y_far = lax.rem(y + 3, 4), lax.rem(y + 1, 4), lax.rem(y + 2, 4)
    y_others = (y_less, y_more, y_far)
    low, high = pl.ds(0, 2), pl.ds(2, 2)
    up, down = at(y + 1, x, c), at(y + 3, x, c)
    right, left = at(y, x + 1, c), at(y, x + 3, c)

    loads[0].wait()
    for i in (1, 3, 2):
        send(TP.at[c, y, x], at(y, x + i, c), gather_recv.at[i - 1])
    send(TP.at[c, y, x], sibling, gather_recv.at[3])
    loads[1].wait()
    for i in (1, 3, 2):
        send(TF.at[y], at(y + i, x, c), gather_recv.at[3 + i])
    for i in (1, 3, 2):
        send(TP.at[c, y, x], at(y + i, x, c), gather_recv.at[6 + i])
    loads[2].wait()
    for i in (1, 3):
        send(SP.at[c, y, x], at(y, x + i, c), gather_recv.at[9 + i])
    loads[3].wait()

    for i in (1, 3, 2):
        block = TP.at[c, y, lax.rem(x + 4 - i, 4)]
        arrived(block, gather_recv.at[i - 1])
        send(block, sibling, gather_recv.at[12 + i])
    for i in (1, 3, 2):
        arrived(TF.at[lax.rem(y + 4 - i, 4)], gather_recv.at[3 + i])

    def score_block(cc, xx):
        j = cc * 4 + xx
        scores = lax.dot_general(
            TF[...].reshape(512, 256), TP[cc, y, xx], NT, preferred_element_type=F32
        )
        K2[j] = scores
        top = jnp.max(scores, axis=0, keepdims=True)
        MC[pl.ds(j, 1), :] = top
        total = jnp.zeros((1, 256), F32)
        for q in range(4):
            e = jnp.exp2((K2[j, q * 128 : q * 128 + 128, :] - top) * KT)
            K2[j, q * 128 : q * 128 + 128, :] = e
            total = total + jnp.sum(e, axis=0, keepdims=True)
        CS[pl.ds(j, 1), :] = total

    @pl.loop(0, 4)
    def _(xx):
        score_block(c, xx)

    pl.semaphore_wait(relay_sem.at[0], 2)
    announce(1, 2)

    arrived(TP.at[1 - c, y, x], gather_recv.at[3])
    for i in (1, 3, 2):
        arrived(TP.at[1 - c, y, lax.rem(x + 4 - i, 4)], gather_recv.at[12 + i])

    @pl.loop(0, 4)
    def _(xx):
        score_block(1 - c, xx)

    C1[xc, 0] = MC[...]
    C1[xc, 1] = CS[...]
    wait_c1 = exchange(C1, xc, xc_group)
    send(SP.at[c, y, x], at(y, x + 2, c), gather_recv.at[11])
    pl.semaphore_wait(relay_sem.at[1], 2)
    announce(2, 4)
    wait_c1()
    for i in (1, 3, 2):
        arrived(TP.at[c, lax.rem(y + 4 - i, 4), x], gather_recv.at[6 + i])
    for k, yy in enumerate(y_others):
        send(TP.at[c, yy, x], right, gather_recv.at[17 + k])
        send(TP.at[c, yy, x], left, gather_recv.at[20 + k])
    top = C1[0, 0]
    for d in range(1, 8):
        top = jnp.maximum(top, C1[d, 0])
    total = jnp.zeros((8, 256), F32)
    for d in range(8):
        total = total + C1[d, 1] * jnp.exp2((C1[d, 0] - top) * KT)
    FS[...] = jnp.exp2((MC[...] - top) * KT)
    MY[y] = top
    wait_my = exchange(MY, y, y_group)
    CE[...] = FS[...] / (PROTOS * total)

    def row_pass(it):
        @pl.loop(0, 8)
        def _(q):
            rows = pl.ds(pl.multiple_of(q * 64, 64), 64)
            acc = jnp.zeros((64, 128), F32)
            for j in range(8):
                acc = acc + halves(K2[j, rows, :] * CE[j : j + 1, :])
            ACC[rows, :] = acc

        for q in range(4):
            RY[it, y, q : q + 1, :] = lane_sums(ACC[q * 128 : q * 128 + 128, :])
        exchange(RY.at[it], y, y_group)()
        r = RY[it, 0]
        for d in range(1, 4):
            r = r + RY[it, d]
        RZ[it, z] = r
        if it == 0:
            pl.semaphore_wait(relay_sem.at[2], 2)
        return exchange(RZ.at[it], z, z_group)

    def row_end(it, wait):
        wait()
        r = RZ[it, 0]
        for d in range(1, 16):
            r = r + RZ[it, d]
        w = 1.0 / (ROWS * r)
        for q in range(4):
            WB[q] = across(w[q : q + 1, :])

    def col_pass(it):
        @pl.loop(0, 8)
        def _(j):
            total = jnp.zeros((1, 256), F32)
            for q in range(4):
                part = K2[j, q * 128 : q * 128 + 128, :] * twice(WB[q])
                total = total + jnp.sum(part, axis=0, keepdims=True)
            CS[pl.ds(j, 1), :] = total

        CB[it, xc] = CS[...] * FS[...]
        return exchange(CB.at[it], xc, xc_group)

    def col_end(it, wait):
        wait()
        total = CB[it, 0]
        for d in range(1, 8):
            total = total + CB[it, d]
        return 1.0 / (PROTOS * total)

    x_far = lax.rem(x + 2, 4)

    def kernel_rows(yy):
        @pl.loop(0, 8)
        def _(j):
            cc, xx = j // 4, lax.rem(j, 4)
            scores = lax.dot_general(TF[y], TP[cc, yy, xx], NT, preferred_element_type=F32)
            KR[(yy * 4 + xx) * 2 + cc] = jnp.exp2((scores - MY[yy, pl.ds(j, 1), :]) * KT)

    def softmax_part(parts):
        old = TOPS[...]
        top = old
        for cc, yy in parts:

            def logit_block(xx, top, cc=cc, yy=yy):
                logits = lax.dot_general(SF[...], SP[cc, yy, xx], NT, preferred_element_type=F32)
                LG[(yy * 4 + xx) * 2 + cc] = logits
                return jnp.maximum(top, jnp.maximum(logits[:, :128], logits[:, 128:]))

            top = lax.fori_loop(0, 4, logit_block, top)
        top = jnp.broadcast_to(jnp.max(top, axis=1, keepdims=True), (128, 128))
        shrink = jnp.exp2((old - top) * KS)
        TOPS[...] = top
        state = SUMS[...] * shrink, SOFT[...] * twice(shrink)
        for cc, yy in parts:

            def softmax_block(xx, carried, cc=cc, yy=yy):
                total, out = carried
                e = jnp.exp2((LG[(yy * 4 + xx) * 2 + cc] - twice(TOPS[...])) * KS)
                return total + halves(e), out + product(e, SP[cc, yy, xx])

            state = lax.fori_loop(0, 4, softmax_block, state)
        SUMS[...], SOFT[...] = state

    TOPS[...] = jnp.full((128, 128), -jnp.inf, F32)
    SUMS[...] = jnp.zeros((128, 128), F32)
    SOFT[...] = jnp.zeros((128, 256), F32)

    wait_row = row_pass(0)
    for i in (1, 3, 2):
        arrived(SP.at[c, y, lax.rem(x + 4 - i, 4)], gather_recv.at[9 + i])
    send(SP.at[c, y], up, gather_recv.at[26])
    send(SP.at[c, y], down, gather_recv.at[27])
    send(SP.at[c, y], sibling, gather_recv.at[16])
    for k, yy in enumerate(y_others):
        send(TP.at[c, yy, x], sibling, gather_recv.at[23 + k])
    kernel_rows(y)
    arrived(SP.at[1 - c, y], gather_recv.at[16])
    softmax_part(((c, y), (1 - c, y)))
    row_end(0, wait_row)
    col = col_end(0, col_pass(0))
    CE[...] = col * FS[...]
    for k, yy in enumerate(y_others):
        arrived(TP.at[c, yy, x_less], gather_recv.at[17 + k])
        arrived(TP.at[c, yy, x_more], gather_recv.at[20 + k])
    for k, yy in enumerate(y_others):
        send(TP.at[c, yy, x_less, pl.ds(0, 128)], right, gather_recv.at[32 + k])
        send(TP.at[c, yy, x_more, pl.ds(128, 128)], left, gather_recv.at[35 + k])

    wait_row = row_pass(1)
    arrived(SP.at[c, y_less], gather_recv.at[26])
    arrived(SP.at[c, y_more], gather_recv.at[27])
    send(SP.at[c, y_less], sibling, gather_recv.at[44])
    send(SP.at[c, y_more], sibling, gather_recv.at[45])
    send(SP.at[c, y_less, low], up, gather_recv.at[30])
    send(SP.at[c, y_more, high], down, gather_recv.at[31])
    softmax_part([(c, y_less), (c, y_more)])
    arrived(SP.at[1 - c, y_less], gather_recv.at[44])
    arrived(SP.at[1 - c, y_more], gather_recv.at[45])
    for k, yy in enumerate(y_others):
        send(TP.at[c, yy, x_less], sibling, gather_recv.at[38 + k])
        send(TP.at[c, yy, x_more], sibling, gather_recv.at[41 + k])
    softmax_part([(1 - c, y_less), (1 - c, y_more)])
    row_end(1, wait_row)
    wait_col = col_pass(1)

    arrived(SP.at[c, y_far, low], gather_recv.at[30])
    arrived(SP.at[c, y_far, high], gather_recv.at[31])
    send(SP.at[c, y_far], sibling, gather_recv.at[48])
    softmax_part([(c, y_far)])
    for k, yy in enumerate(y_others):
        arrived(TP.at[c, yy, x_far, pl.ds(0, 128)], gather_recv.at[32 + k])
        arrived(TP.at[c, yy, x_far, pl.ds(128, 128)], gather_recv.at[35 + k])
    arrived(SP.at[1 - c, y_far], gather_recv.at[48])
    for k, yy in enumerate(y_others):
        send(TP.at[c, yy, x_far], sibling, gather_recv.at[49 + k])
    softmax_part([(1 - c, y_far)])
    ST[z, 0:1, :] = TOPS[...].T[0:1, :]
    ST[z, 1:2, :] = lane_sums(SUMS[...])
    wait_st = exchange(ST, z, z_group)
    BS[...] = SOFT[...].reshape(16, 8, 256)
    wait_b = scatter(BS, BR)

    CY[y] = col_end(1, wait_col)
    wait_cy = exchange(CY, y, y_group)
    wait_my()
    for k, yy in enumerate(y_others):
        arrived(TP.at[1 - c, yy, x], gather_recv.at[23 + k])
        arrived(TP.at[1 - c, yy, x_less], gather_recv.at[38 + k])
        arrived(TP.at[1 - c, yy, x_more], gather_recv.at[41 + k])
        arrived(TP.at[1 - c, yy, x_far], gather_recv.at[49 + k])
    for yy in y_others:
        kernel_rows(yy)

    def plan_part(yy, carried):
        def plan_block(j, carried):
            rsum, out = carried
            cc, xx = j // 4, lax.rem(j, 4)
            g = (yy * 4 + xx) * 2 + cc
            share = KR[g] * CY[yy, pl.ds(j, 1), :]
            KR[g] = share
            return rsum + halves(share), out + product(share, SP[cc, yy, xx])

        return lax.fori_loop(0, 8, plan_block, carried)

    state = plan_part(y, (jnp.zeros((128, 128), F32), jnp.zeros((128, 256), F32)))
    wait_cy()
    for yy in y_others:
        state = plan_part(yy, state)
    rsum, out = state
    RT[z, 0:1, :] = lane_sums(rsum)
    RT[z, 1:2, :] = lane_sums(halves(SF[...].astype(F32) * out) - TOPS[...] * rsum)
    wait_rt = exchange(RT, z, z_group)
    AS[...] = out.reshape(16, 8, 256)
    wait_a = scatter(AS, AR)

    wait_st()
    tops = ST[:, 0, :]
    row_top = jnp.max(tops, axis=0, keepdims=True)
    below = tops - row_top
    scale = jnp.exp2(below * KS)
    row_sum = jnp.sum(ST[:, 1, :] * scale, axis=0, keepdims=True)
    WB[1, :, 0:16] = (scale / row_sum).T
    wait_rt()
    r = jnp.sum(RT[:, 0, :], axis=0, keepdims=True)
    t = jnp.sum(RT[:, 1, :] + RT[:, 0, :] * below, axis=0, keepdims=True)
    weight = 1.0 / r
    part = jnp.log(row_sum) - weight * t * (1.0 / STUDENT_TEMP)
    LY[y] = jnp.broadcast_to(part, (8, 128))
    wait_ly = exchange(LY, y, y_group)
    WB[0] = across(weight)

    mine = pl.ds(pl.multiple_of(z * 8, 8), 8)
    wait_b()
    scale = WB[1, mine, :]
    soft_sum = BR[0] * scale[:, 0:1]
    for d in range(1, 16):
        soft_sum = soft_sum + BR[d] * scale[:, d : d + 1]
    wait_a()
    plan_sum = AR[0]
    for d in range(1, 16):
        plan_sum = plan_sum + AR[d]
    mixed = (soft_sum - twice(WB[0, mine, :]) * plan_sum) / (ROWS * STUDENT_TEMP)
    GS[z] = jnp.concatenate([mixed[:, :128], mixed[:, 128:]], axis=0).astype(BF16)
    wait_gs = exchange(GS, z, z_group)

    writes = []
    for q in range(4):

        @pl.loop(0, 8)
        def _(n):
            g = q * 8 + n
            columns = pl.ds(pl.multiple_of(g * 256, 256), 256)
            TG[:, columns] = (KR[g] * twice(WB[0])).astype(BF16)

        columns = slice(q * 2048, q * 2048 + 2048)
        write = pltpu.make_async_copy(TG.at[:, columns], targets.at[:, columns], out_sem.at[q])
        write.start()
        writes.append(write)

    wait_ly()
    LC[xc] = ((LY[0] + LY[1]) + LY[2]) + LY[3]
    wait_lc = exchange(LC, xc, xc_group)
    wait_lc()
    part = LC[0]
    for d in range(1, 8):
        part = part + LC[d]
    loss[...] = jnp.sum(part, axis=1, keepdims=True)[0:1, :] / ROWS

    wait_gs()
    for d in range(16):
        rows = GS[d].astype(F32)
        grad[d * 8 : d * 8 + 8, :128] = rows[:8]
        grad[d * 8 : d * 8 + 8, 128:] = rows[8:]
    for write in writes:
        write.wait()
    for ref, sem in unsent:
        arrived(ref, sem)


def on_device(teacher_feat, student_feat, teacher_proto, student_proto):
    any_spec = pl.BlockSpec(memory_space=pl.ANY)
    vmem_spec = pl.BlockSpec(memory_space=pltpu.VMEM)

    def f32(*shape):
        return pltpu.VMEM(shape, F32)

    def bf16(*shape):
        return pltpu.VMEM(shape, BF16)

    held = [
        pltpu.with_memory_space_constraint(a, pltpu.HBM)
        for a in (teacher_feat, student_feat, teacher_proto, student_proto)
    ]
    targets, grad, loss = pl.pallas_call(
        kernel,
        out_shape=(
            jax.ShapeDtypeStruct((128, 8192), BF16),
            jax.ShapeDtypeStruct((128, 256), F32),
            jax.ShapeDtypeStruct((1, 1), F32),
        ),
        in_specs=[pl.BlockSpec(memory_space=pltpu.HBM)] * 4,
        out_specs=(any_spec, vmem_spec, vmem_spec),
        scratch_shapes=[
            bf16(4, 128, 256),
            bf16(128, 256),
            bf16(2, 4, 4, 256, 256),
            bf16(2, 4, 4, 256, 256),
            f32(8, 512, 256),
            f32(32, 128, 256),
            f32(32, 128, 256),
            bf16(128, 8192),
            f32(8, 256),
            f32(8, 256),
            f32(8, 256),
            f32(8, 256),
            f32(512, 128),
            f32(4, 128, 128),
            f32(128, 128),
            f32(128, 128),
            f32(128, 256),
            f32(8, 2, 8, 256),
            f32(2, 8, 8, 256),
            f32(2, 4, 4, 128),
            f32(2, 16, 4, 128),
            f32(4, 8, 256),
            f32(4, 8, 256),
            f32(16, 2, 128),
            f32(16, 8, 256),
            f32(16, 8, 256),
            f32(16, 2, 128),
            f32(16, 8, 256),
            f32(16, 8, 256),
            bf16(16, 16, 128),
            f32(4, 8, 128),
            f32(8, 8, 128),
            pltpu.SemaphoreType.REGULAR((3,)),
            pltpu.SemaphoreType.DMA((4,)),
            pltpu.SemaphoreType.DMA((56,)),
            pltpu.SemaphoreType.DMA((56,)),
            pltpu.SemaphoreType.DMA((16,)),
            pltpu.SemaphoreType.DMA((16,)),
            pltpu.SemaphoreType.DMA((4,)),
        ],
        compiler_params=pltpu.CompilerParams(
            collective_id=0, has_side_effects=True, vmem_limit_bytes=48 * 2**20
        ),
        cost_estimate=pl.CostEstimate(
            flops=2_000_000_000, bytes_accessed=4_000_000, transcendentals=4_000_000
        ),
    )(*held)
    return targets, grad, loss.reshape(())


def solution(mesh):
    return jax.shard_map(
        on_device,
        mesh=mesh,
        in_specs=(
            P("batch", None),
            P("batch", None),
            P(("proto", "batch"), None),
            P(("proto", "batch"), None),
        ),
        out_specs=(P("batch", "proto"), P("batch", None), P()),
        check_vma=False,
    )
```

```python
import jax
import jax.numpy as jnp
from jax import lax
from jax.experimental import pallas as pl
from jax.experimental.pallas import tpu as pltpu
from jax.sharding import PartitionSpec as P

PROTOS = 131072
ROWS = 4096
TEACHER_TEMP = 0.07
STUDENT_TEMP = 0.1
LOG2E = 1.4426950408889634
KT = LOG2E / TEACHER_TEMP
KS = LOG2E / STUDENT_TEMP
F32 = jnp.float32
BF16 = jnp.bfloat16
NT = (((1,), (1,)), ((), ()))
Z_ORDER = (8, 7, 9, 6, 10, 5, 11, 4, 12, 3, 13, 2, 14, 1, 15)


def across(row):
    return jnp.broadcast_to(row, (128, 128)).T


def lane_sums(a):
    return jnp.sum(a.T, axis=0, keepdims=True)


def twice(a):
    return jnp.concatenate([a, a], axis=1)


def halves(a):
    return a[:, :128] + a[:, 128:]


def product(values, centers):
    high = values.astype(BF16)
    low = (values - high.astype(F32)).astype(BF16)
    return jnp.dot(high, centers, preferred_element_type=F32) + jnp.dot(
        low, centers, preferred_element_type=F32
    )


def kernel(
    tf, sf, tp, sp,
    targets, grad, loss,
    TF, SF, TP, SP, K2, KR, LG, TG,
    MC, CS, FS, CE, ACC, WB, TOPS, SUMS, SOFT,
    C1, CB, RY, RZ, MY, CY, ST, BS, BR, RT, AS, AR, GS, LY, LC,
    relay_sem, local_sem, gather_send, gather_recv, ex_send, ex_recv, out_sem,
):
    b, z = lax.axis_index("batch"), lax.axis_index("proto")
    y, x, c = b // 8, lax.rem(b // 2, 4), lax.rem(b, 2)
    xc = lax.rem(b, 8)

    def at(y_, x_, c_):
        return {"batch": (lax.rem(y_, 4) * 4 + lax.rem(x_, 4)) * 2 + c_}

    def around(i):
        return {"proto": lax.rem(z + i, 16)}

    sibling = at(y, x, 1 - c)
    y_group = [at(y + i, x, c) for i in (1, 3, 2)]
    xc_group = [{"batch": y * 8 + lax.rem(xc + i, 8)} for i in range(1, 8)]
    z_group = [around(i) for i in Z_ORDER]

    loads = [
        pltpu.make_async_copy(tp, TP.at[c, y, x], local_sem.at[0]),
        pltpu.make_async_copy(tf, TF.at[y], local_sem.at[1]),
        pltpu.make_async_copy(sp, SP.at[c, y, x], local_sem.at[2]),
        pltpu.make_async_copy(sf, SF, local_sem.at[3]),
    ]
    for load in loads:
        load.start()

    barrier = pltpu.get_barrier_semaphore()
    partners = [around(1), around(15)] + xc_group + y_group
    for partner in partners:
        pl.semaphore_signal(barrier, inc=1, device_id=partner)
    pl.semaphore_wait(barrier, len(partners))

    def announce(k, i):
        for step in (i, 16 - i):
            pl.semaphore_signal(relay_sem.at[k], inc=1, device_id=around(step))

    announce(0, 1)

    unsent = []
    used = [0]

    def send(ref, device, recv_sem, dst=None):
        k = used[0]
        used[0] += 1
        copy = pltpu.make_async_remote_copy(
            src_ref=ref,
            dst_ref=ref if dst is None else dst,
            send_sem=gather_send.at[k],
            recv_sem=recv_sem,
            device_id=device,
        )
        copy.start()
        unsent.append((ref, gather_send.at[k]))

    def arrived(ref, sem):
        pltpu.make_async_copy(ref, ref, sem).wait()

    exchanges = [0]

    def exchange(buf, me, group):
        k = exchanges[0]
        exchanges[0] += 1
        for device in group:
            pltpu.make_async_remote_copy(
                src_ref=buf.at[me],
                dst_ref=buf.at[me],
                send_sem=ex_send.at[k],
                recv_sem=ex_recv.at[k],
                device_id=device,
            ).start()
        all_of = buf.at[pl.ds(0, len(group))]
        unsent.append((all_of, ex_send.at[k]))
        return lambda: arrived(all_of, ex_recv.at[k])

    def scatter(src, buf):
        k = exchanges[0]
        exchanges[0] += 1
        for i in Z_ORDER:
            t = lax.rem(z + i, 16)
            pltpu.make_async_remote_copy(
                src_ref=src.at[t],
                dst_ref=buf.at[z],
                send_sem=ex_send.at[k],
                recv_sem=ex_recv.at[k],
                device_id={"proto": t},
            ).start()
        buf[z] = src[z]
        all_of = buf.at[pl.ds(0, 15)]
        unsent.append((all_of, ex_send.at[k]))
        return lambda: arrived(all_of, ex_recv.at[k])

    x_less, x_more = lax.rem(x + 3, 4), lax.rem(x + 1, 4)
    y_less, y_more, y_far = lax.rem(y + 3, 4), lax.rem(y + 1, 4), lax.rem(y + 2, 4)
    y_others = (y_less, y_more, y_far)
    low, high = pl.ds(0, 2), pl.ds(2, 2)
    up, down = at(y + 1, x, c), at(y + 3, x, c)
    right, left = at(y, x + 1, c), at(y, x + 3, c)

    loads[0].wait()
    for i in (1, 3, 2):
        send(TP.at[c, y, x], at(y, x + i, c), gather_recv.at[i - 1])
    send(TP.at[c, y, x], sibling, gather_recv.at[3])
    loads[1].wait()
    for i in (1, 3, 2):
        send(TF.at[y], at(y + i, x, c), gather_recv.at[3 + i])
    for i in (1, 3, 2):
        send(TP.at[c, y, x], at(y + i, x, c), gather_recv.at[6 + i])
    loads[2].wait()
    for i in (1, 3):
        send(SP.at[c, y, x], at(y, x + i, c), gather_recv.at[9 + i])
    loads[3].wait()

    for i in (1, 3, 2):
        block = TP.at[c, y, lax.rem(x + 4 - i, 4)]
        arrived(block, gather_recv.at[i - 1])
        send(block, sibling, gather_recv.at[12 + i])
    for i in (1, 3, 2):
        arrived(TF.at[lax.rem(y + 4 - i, 4)], gather_recv.at[3 + i])

    def score_block(cc, xx):
        j = cc * 4 + xx
        scores = lax.dot_general(
            TF[...].reshape(512, 256), TP[cc, y, xx], NT, preferred_element_type=F32
        )
        K2[j] = scores
        top = jnp.max(scores, axis=0, keepdims=True)
        MC[pl.ds(j, 1), :] = top
        total = jnp.zeros((1, 256), F32)
        for q in range(4):
            e = jnp.exp2((K2[j, q * 128 : q * 128 + 128, :] - top) * KT)
            K2[j, q * 128 : q * 128 + 128, :] = e
            total = total + jnp.sum(e, axis=0, keepdims=True)
        CS[pl.ds(j, 1), :] = total

    @pl.loop(0, 4)
    def _(xx):
        score_block(c, xx)

    pl.semaphore_wait(relay_sem.at[0], 2)
    announce(1, 2)

    arrived(TP.at[1 - c, y, x], gather_recv.at[3])
    for i in (1, 3, 2):
        arrived(TP.at[1 - c, y, lax.rem(x + 4 - i, 4)], gather_recv.at[12 + i])

    @pl.loop(0, 4)
    def _(xx):
        score_block(1 - c, xx)

    C1[xc, 0] = MC[...]
    C1[xc, 1] = CS[...]
    wait_c1 = exchange(C1, xc, xc_group)
    send(SP.at[c, y, x], at(y, x + 2, c), gather_recv.at[11])
    pl.semaphore_wait(relay_sem.at[1], 2)
    announce(2, 4)
    wait_c1()
    for i in (1, 3, 2):
        arrived(TP.at[c, lax.rem(y + 4 - i, 4), x], gather_recv.at[6 + i])
    for k, yy in enumerate(y_others):
        send(TP.at[c, yy, x], right, gather_recv.at[17 + k])
        send(TP.at[c, yy, x], left, gather_recv.at[20 + k])
    top = C1[0, 0]
    for d in range(1, 8):
        top = jnp.maximum(top, C1[d, 0])
    total = jnp.zeros((8, 256), F32)
    for d in range(8):
        total = total + C1[d, 1] * jnp.exp2((C1[d, 0] - top) * KT)
    FS[...] = jnp.exp2((MC[...] - top) * KT)
    MY[y] = top
    wait_my = exchange(MY, y, y_group)
    CE[...] = FS[...] / (PROTOS * total)

    def row_pass(it):
        @pl.loop(0, 8)
        def _(q):
            rows = pl.ds(pl.multiple_of(q * 64, 64), 64)
            acc = jnp.zeros((64, 128), F32)
            for j in range(8):
                acc = acc + halves(K2[j, rows, :] * CE[j : j + 1, :])
            ACC[rows, :] = acc

        for q in range(4):
            RY[it, y, q : q + 1, :] = lane_sums(ACC[q * 128 : q * 128 + 128, :])
        exchange(RY.at[it], y, y_group)()
        r = RY[it, 0]
        for d in range(1, 4):
            r = r + RY[it, d]
        RZ[it, z] = r
        if it == 0:
            pl.semaphore_wait(relay_sem.at[2], 2)
        return exchange(RZ.at[it], z, z_group)

    def row_end(it, wait):
        wait()
        r = RZ[it, 0]
        for d in range(1, 16):
            r = r + RZ[it, d]
        w = 1.0 / (ROWS * r)
        for q in range(4):
            WB[q] = across(w[q : q + 1, :])

    def col_pass(it):
        @pl.loop(0, 8)
        def _(j):
            total = jnp.zeros((1, 256), F32)
            for q in range(4):
                part = K2[j, q * 128 : q * 128 + 128, :] * twice(WB[q])
                total = total + jnp.sum(part, axis=0, keepdims=True)
            CS[pl.ds(j, 1), :] = total

        CB[it, xc] = CS[...] * FS[...]
        return exchange(CB.at[it], xc, xc_group)

    def col_end(it, wait):
        wait()
        total = CB[it, 0]
        for d in range(1, 8):
            total = total + CB[it, d]
        return 1.0 / (PROTOS * total)

    x_far = lax.rem(x + 2, 4)

    def kernel_rows(yy):
        @pl.loop(0, 8)
        def _(j):
            cc, xx = j // 4, lax.rem(j, 4)
            scores = lax.dot_general(TF[y], TP[cc, yy, xx], NT, preferred_element_type=F32)
            KR[(yy * 4 + xx) * 2 + cc] = jnp.exp2((scores - MY[yy, pl.ds(j, 1), :]) * KT)

    def kernel_column(xx):
        @pl.loop(0, 6)
        def _(n):
            cc, yy = n // 3, lax.rem(y + 1 + lax.rem(n, 3), 4)
            scores = lax.dot_general(TF[y], TP[cc, yy, xx], NT, preferred_element_type=F32)
            tops = MY[yy, pl.ds(cc * 4 + xx, 1), :]
            KR[(yy * 4 + xx) * 2 + cc] = jnp.exp2((scores - tops) * KT)

    def softmax_part(parts):
        old = TOPS[...]
        top = old
        for cc, yy in parts:

            def logit_block(xx, top, cc=cc, yy=yy):
                logits = lax.dot_general(SF[...], SP[cc, yy, xx], NT, preferred_element_type=F32)
                LG[(yy * 4 + xx) * 2 + cc] = logits
                return jnp.maximum(top, jnp.maximum(logits[:, :128], logits[:, 128:]))

            top = lax.fori_loop(0, 4, logit_block, top)
        top = jnp.broadcast_to(jnp.max(top, axis=1, keepdims=True), (128, 128))
        shrink = jnp.exp2((old - top) * KS)
        TOPS[...] = top
        state = SUMS[...] * shrink, SOFT[...] * twice(shrink)
        for cc, yy in parts:

            def softmax_block(xx, carried, cc=cc, yy=yy):
                total, out = carried
                e = jnp.exp2((LG[(yy * 4 + xx) * 2 + cc] - twice(TOPS[...])) * KS)
                return total + halves(e), out + product(e, SP[cc, yy, xx])

            state = lax.fori_loop(0, 4, softmax_block, state)
        SUMS[...], SOFT[...] = state

    TOPS[...] = jnp.full((128, 128), -jnp.inf, F32)
    SUMS[...] = jnp.zeros((128, 128), F32)
    SOFT[...] = jnp.zeros((128, 256), F32)

    wait_row = row_pass(0)
    for i in (1, 3, 2):
        arrived(SP.at[c, y, lax.rem(x + 4 - i, 4)], gather_recv.at[9 + i])
    send(SP.at[c, y], up, gather_recv.at[26])
    send(SP.at[c, y], down, gather_recv.at[27])
    send(SP.at[c, y], sibling, gather_recv.at[16])
    for k, yy in enumerate(y_others):
        send(TP.at[c, yy, x], sibling, gather_recv.at[23 + k])
    kernel_rows(y)
    arrived(SP.at[1 - c, y], gather_recv.at[16])
    softmax_part(((c, y), (1 - c, y)))
    wait_my()
    for k, yy in enumerate(y_others):
        arrived(TP.at[1 - c, yy, x], gather_recv.at[23 + k])
    kernel_column(x)
    row_end(0, wait_row)
    col = col_end(0, col_pass(0))
    CE[...] = col * FS[...]
    for k, yy in enumerate(y_others):
        arrived(TP.at[c, yy, x_less], gather_recv.at[17 + k])
        arrived(TP.at[c, yy, x_more], gather_recv.at[20 + k])
    for k, yy in enumerate(y_others):
        send(TP.at[c, yy, x_less, pl.ds(0, 128)], right, gather_recv.at[32 + k])
        send(TP.at[c, yy, x_more, pl.ds(128, 128)], left, gather_recv.at[35 + k])

    wait_row = row_pass(1)
    arrived(SP.at[c, y_less], gather_recv.at[26])
    arrived(SP.at[c, y_more], gather_recv.at[27])
    send(SP.at[c, y_less], sibling, gather_recv.at[44])
    send(SP.at[c, y_more], sibling, gather_recv.at[45])
    send(SP.at[c, y_less, low], up, gather_recv.at[30])
    send(SP.at[c, y_more, high], down, gather_recv.at[31])
    softmax_part([(c, y_less), (c, y_more)])
    arrived(SP.at[1 - c, y_less], gather_recv.at[44])
    arrived(SP.at[1 - c, y_more], gather_recv.at[45])
    for k, yy in enumerate(y_others):
        send(TP.at[c, yy, x_less], sibling, gather_recv.at[38 + k])
        send(TP.at[c, yy, x_more], sibling, gather_recv.at[41 + k])
    softmax_part([(1 - c, y_less), (1 - c, y_more)])
    row_end(1, wait_row)
    wait_col = col_pass(1)

    arrived(SP.at[c, y_far, low], gather_recv.at[30])
    arrived(SP.at[c, y_far, high], gather_recv.at[31])
    send(SP.at[c, y_far], sibling, gather_recv.at[48])
    softmax_part([(c, y_far)])
    for k, yy in enumerate(y_others):
        arrived(TP.at[c, yy, x_far, pl.ds(0, 128)], gather_recv.at[32 + k])
        arrived(TP.at[c, yy, x_far, pl.ds(128, 128)], gather_recv.at[35 + k])
    arrived(SP.at[1 - c, y_far], gather_recv.at[48])
    for k, yy in enumerate(y_others):
        send(TP.at[c, yy, x_far], sibling, gather_recv.at[49 + k])
    softmax_part([(1 - c, y_far)])
    ST[z, 0:1, :] = TOPS[...].T[0:1, :]
    ST[z, 1:2, :] = lane_sums(SUMS[...])
    BS[...] = SOFT[...].reshape(16, 8, 256)

    CY[y] = col_end(1, wait_col)
    wait_cy = exchange(CY, y, y_group)
    wait_b = scatter(BS, BR)
    wait_st = exchange(ST, z, z_group)
    for k, yy in enumerate(y_others):
        arrived(TP.at[1 - c, yy, x_less], gather_recv.at[38 + k])
        arrived(TP.at[1 - c, yy, x_more], gather_recv.at[41 + k])
        arrived(TP.at[1 - c, yy, x_far], gather_recv.at[49 + k])
    for xx in (x_less, x_more, x_far):
        kernel_column(xx)

    def plan_part(yy, carried):
        def plan_block(j, carried):
            rsum, out = carried
            cc, xx = j // 4, lax.rem(j, 4)
            g = (yy * 4 + xx) * 2 + cc
            share = KR[g] * CY[yy, pl.ds(j, 1), :]
            KR[g] = share
            return rsum + halves(share), out + product(share, SP[cc, yy, xx])

        return lax.fori_loop(0, 8, plan_block, carried)

    state = plan_part(y, (jnp.zeros((128, 128), F32), jnp.zeros((128, 256), F32)))
    wait_cy()
    for yy in y_others:
        state = plan_part(yy, state)
    rsum, out = state
    AS[...] = out.reshape(16, 8, 256)
    wait_a = scatter(AS, AR)
    RT[z, 0:1, :] = lane_sums(rsum)
    RT[z, 1:2, :] = lane_sums(halves(SF[...].astype(F32) * out) - TOPS[...] * rsum)
    wait_rt = exchange(RT, z, z_group)

    wait_st()
    tops = ST[:, 0, :]
    row_top = jnp.max(tops, axis=0, keepdims=True)
    below = tops - row_top
    scale = jnp.exp2(below * KS)
    row_sum = jnp.sum(ST[:, 1, :] * scale, axis=0, keepdims=True)
    WB[1, :, 0:16] = (scale / row_sum).T
    wait_rt()
    r = jnp.sum(RT[:, 0, :], axis=0, keepdims=True)
    t = jnp.sum(RT[:, 1, :] + RT[:, 0, :] * below, axis=0, keepdims=True)
    weight = 1.0 / r
    part = jnp.log(row_sum) - weight * t * (1.0 / STUDENT_TEMP)
    LY[y] = jnp.broadcast_to(part, (8, 128))
    wait_ly = exchange(LY, y, y_group)
    WB[0] = across(weight)

    mine = pl.ds(pl.multiple_of(z * 8, 8), 8)
    wait_b()
    scale = WB[1, mine, :]
    soft_sum = BR[0] * scale[:, 0:1]
    for d in range(1, 16):
        soft_sum = soft_sum + BR[d] * scale[:, d : d + 1]
    wait_a()
    plan_sum = AR[0]
    for d in range(1, 16):
        plan_sum = plan_sum + AR[d]
    mixed = (soft_sum - twice(WB[0, mine, :]) * plan_sum) / (ROWS * STUDENT_TEMP)
    GS[z] = jnp.concatenate([mixed[:, :128], mixed[:, 128:]], axis=0).astype(BF16)
    wait_gs = exchange(GS, z, z_group)

    writes = []
    for q in range(4):

        @pl.loop(0, 8)
        def _(n):
            g = q * 8 + n
            columns = pl.ds(pl.multiple_of(g * 256, 256), 256)
            TG[:, columns] = (KR[g] * twice(WB[0])).astype(BF16)

        columns = slice(q * 2048, q * 2048 + 2048)
        write = pltpu.make_async_copy(TG.at[:, columns], targets.at[:, columns], out_sem.at[q])
        write.start()
        writes.append(write)

    wait_ly()
    LC[xc] = ((LY[0] + LY[1]) + LY[2]) + LY[3]
    wait_lc = exchange(LC, xc, xc_group)
    wait_lc()
    part = LC[0]
    for d in range(1, 8):
        part = part + LC[d]
    loss[...] = jnp.sum(part, axis=1, keepdims=True)[0:1, :] / ROWS

    wait_gs()
    for d in range(16):
        rows = GS[d].astype(F32)
        grad[d * 8 : d * 8 + 8, :128] = rows[:8]
        grad[d * 8 : d * 8 + 8, 128:] = rows[8:]
    for write in writes:
        write.wait()
    for ref, sem in unsent:
        arrived(ref, sem)


def on_device(teacher_feat, student_feat, teacher_proto, student_proto):
    any_spec = pl.BlockSpec(memory_space=pl.ANY)
    vmem_spec = pl.BlockSpec(memory_space=pltpu.VMEM)

    def f32(*shape):
        return pltpu.VMEM(shape, F32)

    def bf16(*shape):
        return pltpu.VMEM(shape, BF16)

    held = [
        pltpu.with_memory_space_constraint(a, pltpu.HBM)
        for a in (teacher_feat, student_feat, teacher_proto, student_proto)
    ]
    targets, grad, loss = pl.pallas_call(
        kernel,
        out_shape=(
            jax.ShapeDtypeStruct((128, 8192), BF16),
            jax.ShapeDtypeStruct((128, 256), F32),
            jax.ShapeDtypeStruct((1, 1), F32),
        ),
        in_specs=[pl.BlockSpec(memory_space=pltpu.HBM)] * 4,
        out_specs=(any_spec, vmem_spec, vmem_spec),
        scratch_shapes=[
            bf16(4, 128, 256),
            bf16(128, 256),
            bf16(2, 4, 4, 256, 256),
            bf16(2, 4, 4, 256, 256),
            f32(8, 512, 256),
            f32(32, 128, 256),
            f32(32, 128, 256),
            bf16(128, 8192),
            f32(8, 256),
            f32(8, 256),
            f32(8, 256),
            f32(8, 256),
            f32(512, 128),
            f32(4, 128, 128),
            f32(128, 128),
            f32(128, 128),
            f32(128, 256),
            f32(8, 2, 8, 256),
            f32(2, 8, 8, 256),
            f32(2, 4, 4, 128),
            f32(2, 16, 4, 128),
            f32(4, 8, 256),
            f32(4, 8, 256),
            f32(16, 2, 128),
            f32(16, 8, 256),
            f32(16, 8, 256),
            f32(16, 2, 128),
            f32(16, 8, 256),
            f32(16, 8, 256),
            bf16(16, 16, 128),
            f32(4, 8, 128),
            f32(8, 8, 128),
            pltpu.SemaphoreType.REGULAR((3,)),
            pltpu.SemaphoreType.DMA((4,)),
            pltpu.SemaphoreType.DMA((56,)),
            pltpu.SemaphoreType.DMA((56,)),
            pltpu.SemaphoreType.DMA((16,)),
            pltpu.SemaphoreType.DMA((16,)),
            pltpu.SemaphoreType.DMA((4,)),
        ],
        compiler_params=pltpu.CompilerParams(
            collective_id=0, has_side_effects=True, vmem_limit_bytes=48 * 2**20
        ),
        cost_estimate=pl.CostEstimate(
            flops=2_000_000_000, bytes_accessed=4_000_000, transcendentals=4_000_000
        ),
    )(*held)
    return targets, grad, loss.reshape(())


def solution(mesh):
    return jax.shard_map(
        on_device,
        mesh=mesh,
        in_specs=(
            P("batch", None),
            P("batch", None),
            P(("proto", "batch"), None),
            P(("proto", "batch"), None),
        ),
        out_specs=(P("batch", "proto"), P("batch", None), P()),
        check_vma=False,
    )
```

```python
import jax
import jax.numpy as jnp
from jax import lax
from jax.experimental import pallas as pl
from jax.experimental.pallas import tpu as pltpu
from jax.sharding import PartitionSpec as P

PROTOS = 131072
ROWS = 4096
TEACHER_TEMP = 0.07
STUDENT_TEMP = 0.1
LOG2E = 1.4426950408889634
KT = LOG2E / TEACHER_TEMP
KS = LOG2E / STUDENT_TEMP
F32 = jnp.float32
BF16 = jnp.bfloat16
NT = (((1,), (1,)), ((), ()))
Z_ORDER = (8, 7, 9, 6, 10, 5, 11, 4, 12, 3, 13, 2, 14, 1, 15)


def across(row):
    return jnp.broadcast_to(row, (128, 128)).T


def lane_sums(a):
    return jnp.sum(a.T, axis=0, keepdims=True)


def twice(a):
    return jnp.concatenate([a, a], axis=1)


def halves(a):
    return a[:, :128] + a[:, 128:]


def product(values, centers):
    high = values.astype(BF16)
    low = (values - high.astype(F32)).astype(BF16)
    return jnp.dot(high, centers, preferred_element_type=F32) + jnp.dot(
        low, centers, preferred_element_type=F32
    )


def kernel(
    tf, sf, tp, sp,
    targets, grad, loss,
    TF, SF, TP, SP, K2, KR, LG, TG,
    MC, CS, FS, CE, ACC, WB, TOPS, SUMS, SOFT,
    C1, CB, RY, RZ, MY, CY, ST, BS, BR, RT, AS, AR, GS, LY, LC,
    relay_sem, local_sem, gather_send, gather_recv, ex_send, ex_recv, out_sem,
):
    b, z = lax.axis_index("batch"), lax.axis_index("proto")
    y, x, c = b // 8, lax.rem(b // 2, 4), lax.rem(b, 2)
    xc = lax.rem(b, 8)

    def at(y_, x_, c_):
        return {"batch": (lax.rem(y_, 4) * 4 + lax.rem(x_, 4)) * 2 + c_}

    def around(i):
        return {"proto": lax.rem(z + i, 16)}

    sibling = at(y, x, 1 - c)
    y_group = [at(y + i, x, c) for i in (1, 3, 2)]
    xc_group = [{"batch": y * 8 + lax.rem(xc + i, 8)} for i in range(1, 8)]
    z_group = [around(i) for i in Z_ORDER]

    loads = [
        pltpu.make_async_copy(tp, TP.at[c, y, x], local_sem.at[0]),
        pltpu.make_async_copy(tf, TF.at[y], local_sem.at[1]),
        pltpu.make_async_copy(sp, SP.at[c, y, x], local_sem.at[2]),
        pltpu.make_async_copy(sf, SF, local_sem.at[3]),
    ]
    for load in loads:
        load.start()

    barrier = pltpu.get_barrier_semaphore()
    partners = [around(1), around(15)] + xc_group + y_group
    for partner in partners:
        pl.semaphore_signal(barrier, inc=1, device_id=partner)
    pl.semaphore_wait(barrier, len(partners))

    def announce(k, i):
        for step in (i, 16 - i):
            pl.semaphore_signal(relay_sem.at[k], inc=1, device_id=around(step))

    announce(0, 1)

    unsent = []
    used = [0]

    def send(ref, device, recv_sem, dst=None):
        k = used[0]
        used[0] += 1
        copy = pltpu.make_async_remote_copy(
            src_ref=ref,
            dst_ref=ref if dst is None else dst,
            send_sem=gather_send.at[k],
            recv_sem=recv_sem,
            device_id=device,
        )
        copy.start()
        unsent.append((ref, gather_send.at[k]))

    def arrived(ref, sem):
        pltpu.make_async_copy(ref, ref, sem).wait()

    exchanges = [0]

    def exchange(buf, me, group):
        k = exchanges[0]
        exchanges[0] += 1
        for device in group:
            pltpu.make_async_remote_copy(
                src_ref=buf.at[me],
                dst_ref=buf.at[me],
                send_sem=ex_send.at[k],
                recv_sem=ex_recv.at[k],
                device_id=device,
            ).start()
        all_of = buf.at[pl.ds(0, len(group))]
        unsent.append((all_of, ex_send.at[k]))
        return lambda: arrived(all_of, ex_recv.at[k])

    def scatter(src, buf):
        k = exchanges[0]
        exchanges[0] += 1
        for i in Z_ORDER:
            t = lax.rem(z + i, 16)
            pltpu.make_async_remote_copy(
                src_ref=src.at[t],
                dst_ref=buf.at[z],
                send_sem=ex_send.at[k],
                recv_sem=ex_recv.at[k],
                device_id={"proto": t},
            ).start()
        buf[z] = src[z]
        all_of = buf.at[pl.ds(0, 15)]
        unsent.append((all_of, ex_send.at[k]))
        return lambda: arrived(all_of, ex_recv.at[k])

    x_less, x_more = lax.rem(x + 3, 4), lax.rem(x + 1, 4)
    y_less, y_more, y_far = lax.rem(y + 3, 4), lax.rem(y + 1, 4), lax.rem(y + 2, 4)
    y_others = (y_less, y_more, y_far)
    low, high = pl.ds(0, 2), pl.ds(2, 2)
    up, down = at(y + 1, x, c), at(y + 3, x, c)
    right, left = at(y, x + 1, c), at(y, x + 3, c)

    loads[0].wait()
    for i in (1, 3, 2):
        send(TP.at[c, y, x], at(y, x + i, c), gather_recv.at[i - 1])
    send(TP.at[c, y, x], sibling, gather_recv.at[3])
    loads[1].wait()
    for i in (1, 3, 2):
        send(TF.at[y], at(y + i, x, c), gather_recv.at[3 + i])
    for i in (1, 3, 2):
        send(TP.at[c, y, x], at(y + i, x, c), gather_recv.at[6 + i])
    loads[2].wait()
    for i in (1, 3):
        send(SP.at[c, y, x], at(y, x + i, c), gather_recv.at[9 + i])
    loads[3].wait()

    for i in (1, 3, 2):
        block = TP.at[c, y, lax.rem(x + 4 - i, 4)]
        arrived(block, gather_recv.at[i - 1])
        send(block, sibling, gather_recv.at[12 + i])
    for i in (1, 3, 2):
        arrived(TF.at[lax.rem(y + 4 - i, 4)], gather_recv.at[3 + i])

    def score_block(cc, xx):
        j = cc * 4 + xx
        scores = lax.dot_general(
            TF[...].reshape(512, 256), TP[cc, y, xx], NT, preferred_element_type=F32
        )
        K2[j] = scores
        top = jnp.max(scores, axis=0, keepdims=True)
        MC[pl.ds(j, 1), :] = top
        total = jnp.zeros((1, 256), F32)
        for q in range(4):
            e = jnp.exp2((K2[j, q * 128 : q * 128 + 128, :] - top) * KT)
            K2[j, q * 128 : q * 128 + 128, :] = e
            total = total + jnp.sum(e, axis=0, keepdims=True)
        CS[pl.ds(j, 1), :] = total

    @pl.loop(0, 4)
    def _(xx):
        score_block(c, xx)

    pl.semaphore_wait(relay_sem.at[0], 2)
    announce(1, 2)

    arrived(TP.at[1 - c, y, x], gather_recv.at[3])
    for i in (1, 3, 2):
        arrived(TP.at[1 - c, y, lax.rem(x + 4 - i, 4)], gather_recv.at[12 + i])

    @pl.loop(0, 4)
    def _(xx):
        score_block(1 - c, xx)

    C1[xc, 0] = MC[...]
    C1[xc, 1] = CS[...]
    wait_c1 = exchange(C1, xc, xc_group)
    send(SP.at[c, y, x], at(y, x + 2, c), gather_recv.at[11])
    pl.semaphore_wait(relay_sem.at[1], 2)
    announce(2, 4)
    wait_c1()
    for i in (1, 3, 2):
        arrived(TP.at[c, lax.rem(y + 4 - i, 4), x], gather_recv.at[6 + i])
    for k, yy in enumerate(y_others):
        send(TP.at[c, yy, x], right, gather_recv.at[17 + k])
        send(TP.at[c, yy, x], left, gather_recv.at[20 + k])
    top = C1[0, 0]
    for d in range(1, 8):
        top = jnp.maximum(top, C1[d, 0])
    total = jnp.zeros((8, 256), F32)
    for d in range(8):
        total = total + C1[d, 1] * jnp.exp2((C1[d, 0] - top) * KT)
    FS[...] = jnp.exp2((MC[...] - top) * KT)
    MY[y] = top
    wait_my = exchange(MY, y, y_group)
    CE[...] = FS[...] / (PROTOS * total)

    def row_pass(it):
        @pl.loop(0, 8)
        def _(q):
            rows = pl.ds(pl.multiple_of(q * 64, 64), 64)
            acc = jnp.zeros((64, 128), F32)
            for j in range(8):
                acc = acc + halves(K2[j, rows, :] * CE[j : j + 1, :])
            ACC[rows, :] = acc

        for q in range(4):
            RY[it, y, q : q + 1, :] = lane_sums(ACC[q * 128 : q * 128 + 128, :])
        exchange(RY.at[it], y, y_group)()
        r = RY[it, 0]
        for d in range(1, 4):
            r = r + RY[it, d]
        RZ[it, z] = r
        if it == 0:
            pl.semaphore_wait(relay_sem.at[2], 2)
        return exchange(RZ.at[it], z, z_group)

    def row_end(it, wait):
        wait()
        r = RZ[it, 0]
        for d in range(1, 16):
            r = r + RZ[it, d]
        w = 1.0 / (ROWS * r)
        for q in range(4):
            WB[q] = across(w[q : q + 1, :])

    def col_pass(it):
        @pl.loop(0, 8)
        def _(j):
            total = jnp.zeros((1, 256), F32)
            for q in range(4):
                part = K2[j, q * 128 : q * 128 + 128, :] * twice(WB[q])
                total = total + jnp.sum(part, axis=0, keepdims=True)
            CS[pl.ds(j, 1), :] = total

        CB[it, xc] = CS[...] * FS[...]
        return exchange(CB.at[it], xc, xc_group)

    def col_end(it, wait):
        wait()
        total = CB[it, 0]
        for d in range(1, 8):
            total = total + CB[it, d]
        return 1.0 / (PROTOS * total)

    x_far = lax.rem(x + 2, 4)

    def kernel_rows(yy):
        @pl.loop(0, 8)
        def _(j):
            cc, xx = j // 4, lax.rem(j, 4)
            scores = lax.dot_general(TF[y], TP[cc, yy, xx], NT, preferred_element_type=F32)
            KR[(yy * 4 + xx) * 2 + cc] = jnp.exp2((scores - MY[yy, pl.ds(j, 1), :]) * KT)

    def kernel_column(xx):
        @pl.loop(0, 6)
        def _(n):
            cc, yy = n // 3, lax.rem(y + 1 + lax.rem(n, 3), 4)
            scores = lax.dot_general(TF[y], TP[cc, yy, xx], NT, preferred_element_type=F32)
            tops = MY[yy, pl.ds(cc * 4 + xx, 1), :]
            KR[(yy * 4 + xx) * 2 + cc] = jnp.exp2((scores - tops) * KT)

    def softmax_part(parts):
        old = TOPS[...]
        top = old
        for cc, yy in parts:

            def logit_block(xx, top, cc=cc, yy=yy):
                logits = lax.dot_general(SF[...], SP[cc, yy, xx], NT, preferred_element_type=F32)
                LG[(yy * 4 + xx) * 2 + cc] = logits
                return jnp.maximum(top, jnp.maximum(logits[:, :128], logits[:, 128:]))

            top = lax.fori_loop(0, 4, logit_block, top)
        top = jnp.broadcast_to(jnp.max(top, axis=1, keepdims=True), (128, 128))
        shrink = jnp.exp2((old - top) * KS)
        TOPS[...] = top
        state = SUMS[...] * shrink, SOFT[...] * twice(shrink)
        for cc, yy in parts:

            def softmax_block(xx, carried, cc=cc, yy=yy):
                total, out = carried
                e = jnp.exp2((LG[(yy * 4 + xx) * 2 + cc] - twice(TOPS[...])) * KS)
                return total + halves(e), out + product(e, SP[cc, yy, xx])

            state = lax.fori_loop(0, 4, softmax_block, state)
        SUMS[...], SOFT[...] = state

    TOPS[...] = jnp.full((128, 128), -jnp.inf, F32)
    SUMS[...] = jnp.zeros((128, 128), F32)
    SOFT[...] = jnp.zeros((128, 256), F32)

    wait_row = row_pass(0)
    for i in (1, 3, 2):
        arrived(SP.at[c, y, lax.rem(x + 4 - i, 4)], gather_recv.at[9 + i])
    send(SP.at[c, y], up, gather_recv.at[26])
    send(SP.at[c, y], down, gather_recv.at[27])
    send(SP.at[c, y], sibling, gather_recv.at[16])
    for k, yy in enumerate(y_others):
        send(TP.at[c, yy, x], sibling, gather_recv.at[23 + k])
    kernel_rows(y)
    arrived(SP.at[1 - c, y], gather_recv.at[16])
    softmax_part(((c, y), (1 - c, y)))
    wait_my()
    for k, yy in enumerate(y_others):
        arrived(TP.at[1 - c, yy, x], gather_recv.at[23 + k])
    kernel_column(x)
    row_end(0, wait_row)
    col = col_end(0, col_pass(0))
    CE[...] = col * FS[...]
    for k, yy in enumerate(y_others):
        arrived(TP.at[c, yy, x_less], gather_recv.at[17 + k])
        arrived(TP.at[c, yy, x_more], gather_recv.at[20 + k])
    for k, yy in enumerate(y_others):
        send(TP.at[c, yy, x_less, pl.ds(0, 128)], right, gather_recv.at[32 + k])
        send(TP.at[c, yy, x_more, pl.ds(128, 128)], left, gather_recv.at[35 + k])

    wait_row = row_pass(1)
    arrived(SP.at[c, y_less], gather_recv.at[26])
    arrived(SP.at[c, y_more], gather_recv.at[27])
    send(SP.at[c, y_less], sibling, gather_recv.at[44])
    send(SP.at[c, y_more], sibling, gather_recv.at[45])
    send(SP.at[c, y_less, low], up, gather_recv.at[30])
    send(SP.at[c, y_more, high], down, gather_recv.at[31])
    softmax_part([(c, y_less), (c, y_more)])
    arrived(SP.at[1 - c, y_less], gather_recv.at[44])
    arrived(SP.at[1 - c, y_more], gather_recv.at[45])
    for k, yy in enumerate(y_others):
        send(TP.at[c, yy, x_less], sibling, gather_recv.at[38 + k])
        send(TP.at[c, yy, x_more], sibling, gather_recv.at[41 + k])
    softmax_part([(1 - c, y_less), (1 - c, y_more)])
    row_end(1, wait_row)
    wait_col = col_pass(1)

    arrived(SP.at[c, y_far, low], gather_recv.at[30])
    arrived(SP.at[c, y_far, high], gather_recv.at[31])
    send(SP.at[c, y_far], sibling, gather_recv.at[48])
    softmax_part([(c, y_far)])
    for k, yy in enumerate(y_others):
        arrived(TP.at[c, yy, x_far, pl.ds(0, 128)], gather_recv.at[32 + k])
        arrived(TP.at[c, yy, x_far, pl.ds(128, 128)], gather_recv.at[35 + k])
    arrived(SP.at[1 - c, y_far], gather_recv.at[48])
    for k, yy in enumerate(y_others):
        send(TP.at[c, yy, x_far], sibling, gather_recv.at[49 + k])
    softmax_part([(1 - c, y_far)])
    BS[...] = SOFT[...].reshape(16, 8, 256)
    wait_b = scatter(BS, BR)

    CY[y] = col_end(1, wait_col)
    wait_cy = exchange(CY, y, y_group)
    ST[z, 0:1, :] = TOPS[...].T[0:1, :]
    ST[z, 1:2, :] = lane_sums(SUMS[...])
    wait_st = exchange(ST, z, z_group)
    for k, yy in enumerate(y_others):
        arrived(TP.at[1 - c, yy, x_less], gather_recv.at[38 + k])
        arrived(TP.at[1 - c, yy, x_more], gather_recv.at[41 + k])
        arrived(TP.at[1 - c, yy, x_far], gather_recv.at[49 + k])
    for xx in (x_less, x_more, x_far):
        kernel_column(xx)

    def plan_part(yy, carried):
        def plan_block(j, carried):
            rsum, out = carried
            cc, xx = j // 4, lax.rem(j, 4)
            g = (yy * 4 + xx) * 2 + cc
            share = KR[g] * CY[yy, pl.ds(j, 1), :]
            KR[g] = share
            return rsum + halves(share), out + product(share, SP[cc, yy, xx])

        return lax.fori_loop(0, 8, plan_block, carried)

    state = plan_part(y, (jnp.zeros((128, 128), F32), jnp.zeros((128, 256), F32)))
    wait_cy()
    for yy in y_others:
        state = plan_part(yy, state)
    rsum, out = state
    RT[z, 0:1, :] = lane_sums(rsum)
    RT[z, 1:2, :] = lane_sums(halves(SF[...].astype(F32) * out) - TOPS[...] * rsum)
    wait_rt = exchange(RT, z, z_group)
    AS[...] = out.reshape(16, 8, 256)
    wait_a = scatter(AS, AR)

    wait_st()
    tops = ST[:, 0, :]
    row_top = jnp.max(tops, axis=0, keepdims=True)
    below = tops - row_top
    scale = jnp.exp2(below * KS)
    row_sum = jnp.sum(ST[:, 1, :] * scale, axis=0, keepdims=True)
    WB[1, :, 0:16] = (scale / row_sum).T
    wait_rt()
    r = jnp.sum(RT[:, 0, :], axis=0, keepdims=True)
    t = jnp.sum(RT[:, 1, :] + RT[:, 0, :] * below, axis=0, keepdims=True)
    weight = 1.0 / r
    part = jnp.log(row_sum) - weight * t * (1.0 / STUDENT_TEMP)
    LY[y] = jnp.broadcast_to(part, (8, 128))
    wait_ly = exchange(LY, y, y_group)
    WB[0] = across(weight)

    mine = pl.ds(pl.multiple_of(z * 8, 8), 8)
    wait_b()
    scale = WB[1, mine, :]
    soft_sum = BR[0] * scale[:, 0:1]
    for d in range(1, 16):
        soft_sum = soft_sum + BR[d] * scale[:, d : d + 1]
    wait_a()
    plan_sum = AR[0]
    for d in range(1, 16):
        plan_sum = plan_sum + AR[d]
    mixed = (soft_sum - twice(WB[0, mine, :]) * plan_sum) / (ROWS * STUDENT_TEMP)
    GS[z] = jnp.concatenate([mixed[:, :128], mixed[:, 128:]], axis=0).astype(BF16)
    wait_gs = exchange(GS, z, z_group)

    writes = []
    for q in range(4):

        @pl.loop(0, 8)
        def _(n):
            g = q * 8 + n
            columns = pl.ds(pl.multiple_of(g * 256, 256), 256)
            TG[:, columns] = (KR[g] * twice(WB[0])).astype(BF16)

        columns = slice(q * 2048, q * 2048 + 2048)
        write = pltpu.make_async_copy(TG.at[:, columns], targets.at[:, columns], out_sem.at[q])
        write.start()
        writes.append(write)

    wait_ly()
    LC[xc] = ((LY[0] + LY[1]) + LY[2]) + LY[3]
    wait_lc = exchange(LC, xc, xc_group)
    wait_lc()
    part = LC[0]
    for d in range(1, 8):
        part = part + LC[d]
    loss[...] = jnp.sum(part, axis=1, keepdims=True)[0:1, :] / ROWS

    wait_gs()
    for d in range(16):
        rows = GS[d].astype(F32)
        grad[d * 8 : d * 8 + 8, :128] = rows[:8]
        grad[d * 8 : d * 8 + 8, 128:] = rows[8:]
    for write in writes:
        write.wait()
    for ref, sem in unsent:
        arrived(ref, sem)


def on_device(teacher_feat, student_feat, teacher_proto, student_proto):
    any_spec = pl.BlockSpec(memory_space=pl.ANY)
    vmem_spec = pl.BlockSpec(memory_space=pltpu.VMEM)

    def f32(*shape):
        return pltpu.VMEM(shape, F32)

    def bf16(*shape):
        return pltpu.VMEM(shape, BF16)

    held = [
        pltpu.with_memory_space_constraint(a, pltpu.HBM)
        for a in (teacher_feat, student_feat, teacher_proto, student_proto)
    ]
    targets, grad, loss = pl.pallas_call(
        kernel,
        out_shape=(
            jax.ShapeDtypeStruct((128, 8192), BF16),
            jax.ShapeDtypeStruct((128, 256), F32),
            jax.ShapeDtypeStruct((1, 1), F32),
        ),
        in_specs=[pl.BlockSpec(memory_space=pltpu.HBM)] * 4,
        out_specs=(any_spec, vmem_spec, vmem_spec),
        scratch_shapes=[
            bf16(4, 128, 256),
            bf16(128, 256),
            bf16(2, 4, 4, 256, 256),
            bf16(2, 4, 4, 256, 256),
            f32(8, 512, 256),
            f32(32, 128, 256),
            f32(32, 128, 256),
            bf16(128, 8192),
            f32(8, 256),
            f32(8, 256),
            f32(8, 256),
            f32(8, 256),
            f32(512, 128),
            f32(4, 128, 128),
            f32(128, 128),
            f32(128, 128),
            f32(128, 256),
            f32(8, 2, 8, 256),
            f32(2, 8, 8, 256),
            f32(2, 4, 4, 128),
            f32(2, 16, 4, 128),
            f32(4, 8, 256),
            f32(4, 8, 256),
            f32(16, 2, 128),
            f32(16, 8, 256),
            f32(16, 8, 256),
            f32(16, 2, 128),
            f32(16, 8, 256),
            f32(16, 8, 256),
            bf16(16, 16, 128),
            f32(4, 8, 128),
            f32(8, 8, 128),
            pltpu.SemaphoreType.REGULAR((3,)),
            pltpu.SemaphoreType.DMA((4,)),
            pltpu.SemaphoreType.DMA((56,)),
            pltpu.SemaphoreType.DMA((56,)),
            pltpu.SemaphoreType.DMA((16,)),
            pltpu.SemaphoreType.DMA((16,)),
            pltpu.SemaphoreType.DMA((4,)),
        ],
        compiler_params=pltpu.CompilerParams(
            collective_id=0, has_side_effects=True, vmem_limit_bytes=48 * 2**20
        ),
        cost_estimate=pl.CostEstimate(
            flops=2_000_000_000, bytes_accessed=4_000_000, transcendentals=4_000_000
        ),
    )(*held)
    return targets, grad, loss.reshape(())


def solution(mesh):
    return jax.shard_map(
        on_device,
        mesh=mesh,
        in_specs=(
            P("batch", None),
            P("batch", None),
            P(("proto", "batch"), None),
            P(("proto", "batch"), None),
        ),
        out_specs=(P("batch", "proto"), P("batch", None), P()),
        check_vma=False,
    )
```
